512 devices in a mesh: seq: 128 (over y, z, core), head: 4 (over x).
Axes of the slice: x: 4, y: 8, z: 8, core: 2. Of those that a mesh axis runs over, the one named last changes fastest.
Arguments:
- routed_qkv: bfloat16 [3, 32768, 1024], P(None, 'seq', 'head'), may hold values from -64 to 64
- local_qkv: bfloat16 [3, 32768, 3072], P(None, 'seq', 'head'), may hold values from -64 to 64
- cluster_ids: int32 [8, 32768, 1], P('head', 'seq'), may hold values from 0 to 255; in each aligned block of 256 rows (0 to 255, 256 to 511, ..., all dimensions but the last counted through in order) at most 2 rows name the same one
- wo_routed: bfloat16 [1024, 4096], P('head', 'seq'), may hold values from -0.09375 to 0.09375
- wo_local: bfloat16 [3072, 4096], P('head', 'seq'), may hold values from -0.09375 to 0.09375
Outputs:
- layer_out: bfloat16 [32768, 4096], P('seq', 'head')
The draws below stay inside these ranges and needn't reach their ends.
Inputs may be any that keep to these rules, and one draw needn't show every extreme that they name: `cluster_ids`: in each routed head, no cluster holds more than 2 of the 256 tokens of one index of seq (aligned blocks of 256 rows), and some cluster holds exactly 2 of them.
All inputs are finite; a program needn't handle non-finite values.
Results may differ from the reference program's by a relative error of at most 0.0095.
Values may be sent and summed in bfloat16 or wider, within the bound.
A program may use at most 64 MiB of HBM per device.

```python
import math
import jax
import jax.numpy as jnp
import numpy as np
from jax import lax

D = 4096
HEADS = 32
HD = 128
ROUTED = 8
LOCAL = 24
TOK_DEV = 256
WIN = 256
CLUSTERS = 256
MOST = 2
TOKENS = 32768
N_SEQ = 128
N_HEAD = 4


def make_qkv(key, width):
    base = jax.random.truncated_normal(key, -4.0, 4.0, (3, TOKENS, width), jnp.float32)
    return base.astype(jnp.bfloat16)


def draw_routed_qkv(key, part):
    return make_qkv(jax.random.fold_in(key, 17), ROUTED * HD)


def draw_local_qkv(key, part):
    return make_qkv(jax.random.fold_in(key, 29), LOCAL * HD)


def levels(key, extent, shards, low, high):
    level, own = 1.0, jax.random.fold_in(key, 6)
    for position, parts in shards:
        steps = jnp.exp(jax.random.uniform(jax.random.fold_in(own, position), (parts,), jnp.float32, low / len(shards), high / len(shards)))
        level = level * jnp.repeat(steps, extent[position] // parts).reshape([-1 if axis == position else 1 for axis in range(len(extent))])
    return level


def shared_out(own_key, own, number, rows, count, top, most, skew):
    sequence = jax.random.permutation(own_key, count)
    heavy_load, common = shares(count, rows * top, most, skew, True), shares(count, rows * top, most, skew, False)
    places = jnp.arange(count)

    def named(sizes, offset_by):
        used = int((sizes > 0).sum())
        fixed = max(1, used // 4)
        shifted = fixed + (places - fixed + offset_by * (used - fixed)) % max(1, count - fixed)
        return jnp.zeros((count,), jnp.int32).at[sequence[jnp.where(places < fixed, places, shifted)]].set(jnp.asarray(sizes, jnp.int32))

    sizes = jnp.where(number % 4 == 0, named(heavy_load, number // 4), named(common, number - number // 4 - 1))
    mixed = jax.random.permutation(jax.random.fold_in(own, 3), count)
    donor, sink = mixed[0:count // 2 * 2:2], mixed[1:count // 2 * 2:2]
    margin = jnp.minimum(sizes[donor] - 1, most - sizes[sink]) // 2
    margin = jnp.where((donor == sequence[0]) | (sink == sequence[0]) | (sizes[sink] == 0), 0, jnp.maximum(margin, 0))
    shifted = jax.random.randint(jax.random.fold_in(own, 4), (count // 2,), 0, 1 << 20) % (margin + 1)
    sizes = sizes.at[donor].add(-shifted).at[sink].add(shifted)
    items = jnp.searchsorted(jnp.cumsum(sizes), jnp.arange(rows * top), side="right").astype(jnp.int32)
    grid = items.reshape(top, rows).T
    grid = grid[jax.random.permutation(jax.random.fold_in(own, 1), rows)]
    offset_by = jax.random.randint(jax.random.fold_in(own, 2), (rows, 1), 0, top)
    return jnp.take_along_axis(grid, (jnp.arange(top)[None, :] + offset_by) % top, axis=1)


def shares(amount, total, reach, slope, full):
    weights = [(1 << 20) // math.isqrt(grade ** slope) + 1 for grade in range(1, amount + 1)]
    largest = reach if full else min(reach, max(-(-total // amount), total * weights[0] // sum(weights)))
    least = 1 if total - largest >= amount - 1 else 0
    given, spare = [largest] + [least] * (amount - 1), total - largest - least * (amount - 1)
    while spare > 0:
        movable = [i for i in range(1, amount) if given[i] < largest] or [i for i in range(1, amount) if given[i] < reach]
        whole, left = sum([weights[i] for i in movable]), spare
        for i in movable:
            addition = min(reach - given[i], max(1, left * weights[i] // whole), spare)
            given[i] = given[i] + addition
            spare = spare - addition
    return np.array(given)


def normal_values(own_key, dims, deviation, limit, pieces=(), kind=jnp.bfloat16):
    array = deviation * jax.random.normal(own_key, dims, jnp.float32)
    if pieces:
        array = array * levels(own_key, dims, pieces, -0.22, 0.18)
    return jnp.clip(array, -limit, limit).astype(kind)


def setup_inputs(seed: int = 0) -> dict:
    key_of = jax.random.split(jax.random.key(seed), 6)
    routed_qkv = draw_routed_qkv(jax.random.fold_in(key_of[5], 71), 0)
    local_qkv = draw_local_qkv(jax.random.fold_in(key_of[5], 71), 0)
    cluster_ids_keys = jax.random.split(jax.random.fold_in(key_of[2], 1), ROUTED * TOKENS // TOK_DEV)
    cluster_ids_turns = jax.random.permutation(jax.random.fold_in(key_of[2], 3), ROUTED * TOKENS // TOK_DEV)
    cluster_ids = jax.vmap(lambda own, number: shared_out(jax.random.fold_in(key_of[2], 2), own, number, TOK_DEV, CLUSTERS, 1, MOST, 2))(cluster_ids_keys, cluster_ids_turns).reshape((ROUTED, TOKENS, 1))
    wo_routed = normal_values(key_of[3], (ROUTED * HD, D), (HEADS * HD) ** -0.5, 0.09375, ((0, 4), (1, 128)))
    wo_local = normal_values(key_of[4], (LOCAL * HD, D), (HEADS * HD) ** -0.5, 0.09375, ((0, 4), (1, 128)))
    return dict(routed_qkv=routed_qkv, local_qkv=local_qkv, cluster_ids=cluster_ids, wo_routed=wo_routed, wo_local=wo_local)


def attend(query, keys, values, allowed):
    scores = jnp.einsum('...qd,...kd->...qk', query.astype(jnp.float32), keys.astype(jnp.float32)) * (1.0 / math.sqrt(HD))
    scores = jnp.where(allowed, scores, jnp.float32(-1e+30))
    largest = lax.optimization_barrier(jnp.max(scores, axis=-1, keepdims=True))
    raised = jnp.exp(scores - largest)
    weights = (raised / lax.optimization_barrier(jnp.sum(raised, axis=-1, keepdims=True))).astype(jnp.bfloat16)
    return jnp.einsum('...qk,...kd->...qd', weights.astype(jnp.float32), values.astype(jnp.float32)).astype(jnp.bfloat16)

def routed_head(packed):
    qkv_head, cluster = packed
    blocks = cluster.reshape(N_SEQ, TOK_DEV)
    labels = jnp.arange(CLUSTERS, dtype=jnp.int32)
    onehot = (blocks[:, :, None] == labels[None, None, :]).astype(jnp.int32)
    rank = lax.optimization_barrier(jnp.sum((jnp.cumsum(onehot, axis=1) - 1) * onehot, axis=2))
    source = jnp.arange(N_SEQ, dtype=jnp.int32)[:, None]
    flat = (blocks * (N_SEQ * MOST) + source * MOST + rank).reshape(TOKENS).astype(jnp.int32)
    members = jnp.full((CLUSTERS * N_SEQ * MOST,), -1, jnp.int32).at[flat].set(jnp.arange(TOKENS, dtype=jnp.int32))
    members = members.reshape(CLUSTERS, N_SEQ * MOST)
    safe_ids = jnp.maximum(members, 0)
    query = qkv_head[0][safe_ids]
    keys = qkv_head[1][safe_ids]
    values = qkv_head[2][safe_ids]
    allowed = (members[:, None, :] >= 0) & (members[:, None, :] <= members[:, :, None])
    result = attend(query, keys, values, allowed)
    return result.reshape(CLUSTERS * N_SEQ * MOST, HD)[flat]

def window_stack(values_in, blocks):
    padded = jnp.concatenate([jnp.zeros((WIN, HD), values_in.dtype), values_in], axis=0)
    return jnp.concatenate([padded[:-WIN].reshape(blocks, WIN, HD), values_in.reshape(blocks, WIN, HD)], axis=1)

def local_head(qkv_head):
    blocks = TOKENS // WIN
    query = qkv_head[0].reshape(blocks, WIN, HD)
    keys = window_stack(qkv_head[1], blocks)
    values = window_stack(qkv_head[2], blocks)
    offs_query = jnp.arange(WIN, dtype=jnp.int32)[None, :, None]
    offs_key = jnp.arange(2 * WIN, dtype=jnp.int32)[None, None, :] - WIN
    begins = (jnp.arange(blocks, dtype=jnp.int32) * WIN)[:, None, None]
    allowed = (offs_key <= offs_query) & (offs_key > offs_query - WIN) & (begins + offs_key >= 0)
    return attend(query, keys, values, allowed).reshape(TOKENS, HD)

def reference(routed_qkv, local_qkv, cluster_ids, wo_routed, wo_local):
    routed_heads = routed_qkv.reshape(3, TOKENS, ROUTED, HD).transpose(2, 0, 1, 3)
    routed_attn = lax.map(routed_head, (routed_heads, cluster_ids[:, :, 0]))
    routed_attn = routed_attn.transpose(1, 0, 2).reshape(TOKENS, ROUTED * HD)
    local_heads = local_qkv.reshape(3, TOKENS, LOCAL, HD).transpose(2, 0, 1, 3)
    local_attn = lax.map(local_head, local_heads)
    local_attn = local_attn.transpose(1, 0, 2).reshape(TOKENS, LOCAL * HD)
    routed_cols = ROUTED // N_HEAD * HD
    local_cols = LOCAL // N_HEAD * HD
    total = jnp.zeros((TOKENS, D), jnp.float32)
    for group in range(N_HEAD):
        part_sum = jnp.dot(routed_attn[:, group * routed_cols:(group + 1) * routed_cols], wo_routed[group * routed_cols:(group + 1) * routed_cols], preferred_element_type=jnp.float32)
        part_sum = part_sum + jnp.dot(local_attn[:, group * local_cols:(group + 1) * local_cols], wo_local[group * local_cols:(group + 1) * local_cols], preferred_element_type=jnp.float32)
        total = total + part_sum.astype(jnp.bfloat16).astype(jnp.float32)
    return total.astype(jnp.bfloat16)
```

```python
import math

import jax
import jax.numpy as jnp
from jax import lax
from jax.sharding import PartitionSpec as P

HD = 128
WIN = 256
CL_DEV = 2
EMPTY = 128.0


def shifted(block, axis, distance):
    devices = range(lax.axis_size(axis))
    route = [(i - distance, i) for i in devices if i - distance in devices]
    return lax.ppermute(block, axis, route)


def attend(query, keys, values, allowed):
    scores = jnp.einsum("...qd,...kd->...qk", query, keys, preferred_element_type=jnp.float32) * (
        1.0 / math.sqrt(HD)
    )
    scores = jnp.where(allowed, scores, jnp.float32(-1e30))
    largest = jnp.max(scores, axis=-1, keepdims=True)
    raised = jnp.exp(scores - largest)
    weights = (raised / jnp.sum(raised, axis=-1, keepdims=True)).astype(jnp.bfloat16)
    return jnp.einsum(
        "...qk,...kd->...qd", weights, values, preferred_element_type=jnp.float32
    ).astype(jnp.bfloat16)


def on_device(routed_qkv, local_qkv, cluster_ids, wo_routed, wo_local):
    seq_count = lax.axis_size("seq")
    seq_place = lax.axis_index("seq")
    tok_rows = routed_qkv.shape[1]
    routed_count = cluster_ids.shape[0]
    local_count = local_qkv.shape[2] // HD
    cluster_total = CL_DEV * seq_count
    most_slots = max(2, 2 * tok_rows // cluster_total)
    proj_rows = jnp.concatenate([wo_routed, wo_local], axis=0)
    head_rows = (
        routed_qkv.reshape(3, tok_rows, routed_count, HD)
        .transpose(2, 1, 0, 3)
        .reshape(routed_count, tok_rows, 3 * HD)
    )
    cluster = cluster_ids[:, :, 0]
    order = jnp.arange(tok_rows, dtype=jnp.int32)
    same = (cluster[:, :, None] == cluster[:, None, :]) & (order[None, None, :] < order[None, :, None])
    rank = jnp.sum(same.astype(jnp.int32), axis=2)
    slot_index = cluster * most_slots + rank
    slot_total = cluster_total * most_slots
    slot_names = jnp.arange(slot_total, dtype=jnp.int32)
    place = (slot_names[None, :, None] == slot_index[:, None, :]).astype(jnp.bfloat16)
    filled = jnp.sum(place.astype(jnp.float32), axis=2, keepdims=True)
    send_rows = (
        jnp.einsum("hst,htd->hsd", place, head_rows, preferred_element_type=jnp.float32)
        + (1.0 - filled) * EMPTY
    ).astype(jnp.bfloat16)
    rows = lax.all_to_all(send_rows, "seq", split_axis=1, concat_axis=1, tiled=True)
    count = rows.shape[0]
    slots = rows.shape[1]
    group = seq_count * most_slots
    members = (
        rows.reshape(count, seq_count, CL_DEV, most_slots, 3 * HD)
        .transpose(0, 2, 1, 3, 4)
        .reshape(count, CL_DEV, group, 3 * HD)
    )
    present = members[..., HD] < EMPTY / 2
    slot_order = jnp.arange(group, dtype=jnp.int32)
    allowed = present[..., None, :] & (slot_order[None, :] <= slot_order[:, None])
    result = attend(members[..., :HD], members[..., HD : 2 * HD], members[..., 2 * HD :], allowed)
    answered = (
        result.reshape(count, CL_DEV, seq_count, most_slots, HD)
        .transpose(0, 2, 1, 3, 4)
        .reshape(count, slots, HD)
    )
    returned = lax.all_to_all(answered, "seq", split_axis=1, concat_axis=1, tiled=True)
    picked = jnp.einsum(
        "hst,hsd->htd", place, returned, preferred_element_type=jnp.float32
    ).astype(jnp.bfloat16)
    routed_attn = picked.transpose(1, 0, 2).reshape(tok_rows, routed_count * HD)
    heads = local_qkv.reshape(3, tok_rows, local_count, HD).transpose(0, 2, 1, 3)
    tail = jnp.stack([heads[1], heads[2]])
    earlier = shifted(tail, "seq", 1)
    keys = jnp.concatenate([earlier[0], heads[1]], axis=1)
    values = jnp.concatenate([earlier[1], heads[2]], axis=1)
    key_pos = seq_place * tok_rows - WIN + jnp.arange(WIN + tok_rows, dtype=jnp.int32)
    query_pos = seq_place * tok_rows + jnp.arange(tok_rows, dtype=jnp.int32)
    allowed = (
        (key_pos[None, :] >= 0)
        & (key_pos[None, :] <= query_pos[:, None])
        & (key_pos[None, :] > query_pos[:, None] - WIN)
    )
    result = attend(heads[0], keys, values, allowed[None])
    local_attn = result.transpose(1, 0, 2).reshape(tok_rows, local_count * HD)
    joined = jnp.concatenate([routed_attn, local_attn], axis=1)
    terms = jnp.dot(
        joined,
        lax.all_gather(proj_rows, "seq", axis=1, tiled=True),
        preferred_element_type=jnp.float32,
    )
    rounded = terms.astype(jnp.bfloat16)
    return (
        lax.psum_scatter(rounded, "head", scatter_dimension=1, tiled=True)
        .astype(jnp.float32)
        .astype(jnp.bfloat16)
    )


def solution(mesh):
    placed = (
        P(None, "seq", "head"),
        P(None, "seq", "head"),
        P("head", "seq", None),
        P("head", "seq"),
        P("head", "seq"),
    )
    return jax.shard_map(
        on_device, mesh=mesh, in_specs=placed, out_specs=P("seq", "head"), check_vma=False
    )
```

```python
import functools
import math

import jax
import jax.numpy as jnp
from jax import lax
from jax.experimental import pallas as pl
from jax.experimental.pallas import tpu as pltpu
from jax.sharding import PartitionSpec as P

HD = 128
TOK = 256
LOCAL = 6
SIDE = 8
GROUPS = 4
EMPTY = 128.0
NEVER = -1e30
SCALE = 1.0 / math.sqrt(HD)
BF = jnp.bfloat16
F32 = jnp.float32
I32 = jnp.int32
NT = (((1,), (1,)), ((), ()))
NN = (((1,), (0,)), ((), ()))
TN = (((0,), (0,)), ((), ()))


def dot(a, b, dims):
    return lax.dot_general(a, b, dims, preferred_element_type=F32)


def iota(shape, axis):
    return lax.broadcasted_iota(I32, shape, axis)


def div(a, b):
    return lax.div(a, jnp.int32(b))


def rem(a, b):
    return lax.rem(a, jnp.int32(b))


def kernel(
    routed, local, code, wr, wl, out,
    own_x, own_code, place, sent, via, got, answer, back, final, picked, routed_out, acts, halo,
    turned_w, wt, stage_a, stage_b, arrived,
    a0_s, a0_r, halo_s, halo_r, wx_s, wx_r, p1_s, p1_r, p2_s, p2_r, w1_s, w1_r,
    ring_s, ring_r, sib_s, sib_r, q1_s, q1_r, q2_s, q2_r, ax_s, ax_r, xa_s, xa_r, xb_s, xb_r,
):
    h = lax.axis_index("head")
    s = lax.axis_index("seq")
    c = rem(s, 2)
    oc = 1 - c
    chip = div(s, 2)
    z = rem(chip, SIDE)
    y = div(chip, SIDE)
    u = z * oc + y * c
    w = y * oc + z * c
    sibling = s + 1 - 2 * c

    def seq_yz(yy, zz):
        return (yy * SIDE + zz) * 2 + c

    def seq_uw(uu, ww):
        return seq_yz(ww * oc + uu * c, uu * oc + ww * c)

    def to_seq(src, dst, ss, rs, seq):
        return pltpu.make_async_remote_copy(
            src_ref=src, dst_ref=dst, send_sem=ss, recv_sem=rs,
            device_id={"seq": seq}, device_id_type=pl.DeviceIdType.MESH,
        )

    def to_head(src, dst, ss, rs, head):
        return pltpu.make_async_remote_copy(
            src_ref=src, dst_ref=dst, send_sem=ss, recv_sem=rs,
            device_id={"head": head}, device_id_type=pl.DeviceIdType.MESH,
        )

    barrier = pltpu.get_barrier_semaphore()
    for j in range(1, SIDE):
        for target in (seq_uw(rem(u + j, SIDE), w), seq_uw(u, rem(w + j, SIDE))):
            pl.semaphore_signal(barrier, inc=1, device_id={"seq": target}, device_id_type=pl.DeviceIdType.MESH)
    pl.semaphore_signal(barrier, inc=1, device_id={"seq": sibling}, device_id_type=pl.DeviceIdType.MESH)
    for j in range(1, GROUPS):
        pl.semaphore_signal(
            barrier, inc=1, device_id={"head": rem(h + j, GROUPS)}, device_id_type=pl.DeviceIdType.MESH
        )

    @pl.when((c == 0) & (s > 0))
    def _():
        pl.semaphore_signal(barrier, inc=1, device_id={"seq": s - 1}, device_id_type=pl.DeviceIdType.MESH)

    pl.semaphore_wait(barrier, 2 * (SIDE - 1) + 1 + GROUPS - 1 + c * (1 - div(s, 2 * SIDE * SIDE - 1)))

    a0 = [
        to_seq(
            routed.at[j, :, pl.ds(pl.multiple_of(oc * HD, HD), HD)],
            own_x.at[c, :, pl.ds(j * HD, HD)],
            a0_s.at[j], a0_r.at[j], sibling,
        )
        for j in range(3)
    ]
    a0.append(to_seq(code.at[oc], own_code.at[c], a0_s.at[3], a0_r.at[3], sibling))
    for copy in a0:
        copy.start()
    halo_copy = to_seq(local.at[pl.ds(1, 2)], halo, halo_s, halo_r, s + 1)

    @pl.when(s < 2 * SIDE * SIDE - 1)
    def _():
        halo_copy.start()

    for core in range(2):

        @pl.when(c == core)
        def _():
            for j in range(3):
                own_x[core, :, j * HD : (j + 1) * HD] = routed[j, :, core * HD : (core + 1) * HD]
            own_code[core] = code[core]

    def block_of(yy, zz):
        return wt.at[
            div(yy, 2), rem(yy, 2), div(zz, 4), rem(div(zz, 2), 2),
            pl.ds(pl.multiple_of(rem(zz, 2) * 64, 64), 64),
        ]

    def part_of(core):
        return wt.at[
            div(y, 2), rem(y, 2), div(z, 4), rem(div(z, 2), 2),
            pl.ds(pl.multiple_of(rem(z, 2) * 64 + core * 32, 32), 32),
        ]

    def holder(yy, zz):
        return rem(yy + div(zz, 2), 2)

    eye = (iota((32, 32), 0) == iota((32, 32), 1)).astype(F32).astype(BF)
    own_rows = jnp.concatenate([dot(eye, wr[...], NT), dot(eye, wl[...], NT)], axis=1).astype(BF)
    holds = holder(y, z) == c
    wx_send = to_seq(turned_w, part_of(c), wx_s, wx_r, sibling)
    wx_recv = to_seq(turned_w, part_of(oc), wx_s, wx_r, sibling)

    @pl.when(holds)
    def _():
        part_of(c)[...] = own_rows

    @pl.when(jnp.logical_not(holds))
    def _():
        turned_w[...] = own_rows
        wx_send.start()

    for j in range(3):
        to_seq(
            routed.at[j, :, pl.ds(pl.multiple_of(oc * HD, HD), HD)],
            own_x.at[oc, :, pl.ds(j * HD, HD)],
            a0_s.at[j], a0_r.at[j], sibling,
        ).wait_recv()
    to_seq(code.at[oc], own_code.at[oc], a0_s.at[3], a0_r.at[3], sibling).wait_recv()

    def rows_of(b):
        value = own_code[b]
        rank = value & 1
        cluster = value >> 1
        owner = cluster >> 2
        turned = (owner & 7) * SIDE + (owner >> 3)
        goes = turned * oc + owner * c
        return goes * 16 + b * 8 + (cluster & 3) * 2 + rank

    slot = jnp.concatenate([rows_of(0), rows_of(1)], axis=1)[0:1]
    both = own_x[...].reshape(2 * TOK, 3 * HD)
    ones = jnp.ones((2 * TOK, HD), BF)
    for i in range(4):
        hot = (iota((256, 2 * TOK), 0) + i * 256 == slot).astype(F32).astype(BF)
        place[i * 256 : (i + 1) * 256] = hot
        rows = dot(hot, both, NN)
        filled = dot(hot, ones, NN)
        lead = (1.0 - filled) * EMPTY
        rows = jnp.concatenate([rows[:, :HD], rows[:, HD : 2 * HD] + lead, rows[:, 2 * HD :]], axis=1)
        sent[2 * i : 2 * i + 2] = rows.astype(BF).reshape(2, SIDE, 16, 3 * HD)

    def p1(j, sending):
        there, here = rem(u + j, SIDE), rem(u + SIDE - j, SIDE)
        dst = via.at[u] if sending else via.at[here]
        return to_seq(sent.at[there], dst, p1_s.at[j], p1_r.at[j], seq_uw(there, w))

    for j in range(1, SIDE):
        p1(j, True).start()
    via[u] = sent[u]

    def w1(j, core, sending):
        if core == 0:
            target = seq_yz(y, rem(z + j, SIDE))
            blk = block_of(y, z) if sending else block_of(y, rem(z + SIDE - j, SIDE))
        else:
            target = seq_yz(rem(y + j, SIDE), z)
            blk = block_of(y, z) if sending else block_of(rem(y + SIDE - j, SIDE), z)
        return to_seq(blk, blk, w1_s.at[j], w1_r.at[j], target)

    @pl.when(holds)
    def _():
        wx_recv.wait_recv()
        for core in range(2):

            @pl.when(c == core)
            def _():
                for j in range(1, SIDE):
                    w1(j, core, True).start()

    for j in range(1, SIDE):
        p1(j, False).wait_recv()

    def p2(j, sending):
        there, here = rem(w + j, SIDE), rem(w + SIDE - j, SIDE)
        dst = got.at[w] if sending else got.at[here]
        return to_seq(via.at[:, there], dst, p2_s.at[j], p2_r.at[j], seq_uw(u, there))

    for j in range(1, SIDE):
        p2(j, True).start()
    for i in range(SIDE):
        got[w, i] = via[i, w]

    for core in range(2):

        @pl.when(c == core)
        def _():
            for j in range(1, SIDE):
                if core == 0:
                    is_source = holder(y, rem(z + SIDE - j, SIDE)) == 0
                else:
                    is_source = holder(rem(y + SIDE - j, SIDE), z) == 1

                @pl.when(is_source)
                def _():
                    w1(j, core, False).wait_recv()

    def blocks(core, place_on):
        at = rem(place_on + SIDE, SIDE)
        if core == 0:
            return wt.at[div(at, 2), rem(at, 2), :, rem(at, 2)]
        par = rem(div(at, 2), 2)
        return wt.at[:, 1 - par, div(at, 4), par, pl.ds(pl.multiple_of(rem(at, 2) * 64, 64), 64)]

    def half(ref, k, way):
        return ref.at[:, :, pl.ds(way * 512, 512)] if k == SIDE // 2 else ref

    def ring(k, way, core, sending):
        coord = y if core == 0 else z
        sign = 1 - 2 * way
        if sending:
            blk = blocks(core, coord - sign * (k - 1))
        else:
            blk = blocks(core, coord - sign * k)
        blk = half(blk, k, way)
        to = rem(coord + sign + SIDE, SIDE)
        target = seq_yz(to, z) if core == 0 else seq_yz(y, to)
        return to_seq(blk, blk, ring_s.at[k, way], ring_r.at[k, way], target)

    def sib(k, way, path):
        coord = y if path == 0 else z
        blk = blocks(path, coord - (1 - 2 * way) * k)
        return to_seq(blk, blk, sib_s.at[k, way], sib_r.at[k, way], sibling)

    def ways(k):
        return (0,) if k in (0, SIDE // 2) else (0, 1)

    def by_core(body):
        for core in range(2):
            pl.when(c == core)(functools.partial(body, core))

    def ring_step(k):
        def body(core):
            if k > 1:
                for way in range(2):
                    ring(k - 1, way, core, False).wait_recv()
            if k <= SIDE // 2:
                for way in range(2):
                    ring(k, way, core, True).start()
            for way in ways(k - 1):
                sib(k - 1, way, core).start()

        by_core(body)

    def sib_wait(k):
        def body(core):
            for way in ways(k):
                sib(k, way, 1 - core).wait_recv()

        by_core(body)

    ring_step(1)

    @pl.when(s > 0)
    def _():
        halo_copy.wait_recv()

    @pl.when(s == 0)
    def _():
        halo[...] = jnp.zeros_like(halo)

    own_side = iota((TOK, TOK), 1) <= iota((TOK, TOK), 0)
    shift = jnp.where(s > 0, jnp.float32(0.0), jnp.float32(NEVER))
    for n in range(LOCAL):
        cols = slice(n * HD, (n + 1) * HD)
        query = local[0, :, cols]
        here = dot(query, local[1, :, cols], NT) * SCALE
        before = dot(query, halo[0, :, cols], NT) * SCALE + shift
        scores = jnp.where(own_side, here, before)
        raised = jnp.exp(scores - jnp.max(scores, axis=1, keepdims=True))
        weights = raised / jnp.sum(raised, axis=1, keepdims=True)
        near = jnp.where(own_side, weights, 0.0).astype(BF)
        far = jnp.where(own_side, 0.0, weights).astype(BF)
        result = dot(near, local[2, :, cols], NN) + dot(far, halo[1, :, cols], NN)
        acts[:, (2 + n) * HD : (3 + n) * HD] = result.astype(BF)

    for j in range(1, SIDE):
        p2(j, False).wait_recv()

    def code_of(r):
        first, second = (r >> 7) & 7, (r >> 4) & 7
        place_of = (first * SIDE + second) * oc + (second * SIDE + first) * c
        return ((r >> 1) & 3) * 4096 + place_of * 4 + ((r >> 3) & 1) * 2 + (r & 1)

    keys = got[:, :, :, HD : 2 * HD].reshape(1024, HD)
    values = got[:, :, :, 2 * HD :].reshape(1024, HD)
    lane_zero = (iota((8, HD), 1) == 0).astype(F32).astype(BF)
    lead_key = dot(lane_zero, keys, NT)[0:1]
    key_code = jnp.where(lead_key < 0.75 * EMPTY, code_of(iota((8, 1024), 1))[0:1], 1 << 20)
    for i in range(4):
        query = got[2 * i : 2 * i + 2, :, :, 0:HD].reshape(256, HD)
        scores = dot(query, keys, NT) * SCALE
        ahead = code_of(iota((256, HD), 0) + i * 256)[:, 0:1] - key_code
        scores = jnp.where((ahead >= 0) & (ahead < 256), scores, NEVER)
        raised = jnp.exp(scores - jnp.max(scores, axis=1, keepdims=True))
        weights = (raised / jnp.sum(raised, axis=1, keepdims=True)).astype(BF)
        answer[2 * i : 2 * i + 2] = dot(weights, values, NN).astype(BF).reshape(2, SIDE, 16, HD)

    def q1(j, sending):
        there, here = rem(w + j, SIDE), rem(w + SIDE - j, SIDE)
        dst = back.at[w] if sending else back.at[here]
        return to_seq(answer.at[there], dst, q1_s.at[j], q1_r.at[j], seq_uw(u, there))

    for j in range(1, SIDE):
        q1(j, True).start()
    back[w] = answer[w]

    ring_step(2)

    for j in range(1, SIDE):
        q1(j, False).wait_recv()

    def q2(j, sending):
        there, here = rem(u + j, SIDE), rem(u + SIDE - j, SIDE)
        dst = final.at[u] if sending else final.at[here]
        return to_seq(back.at[:, there], dst, q2_s.at[j], q2_r.at[j], seq_uw(there, w))

    for j in range(1, SIDE):
        q2(j, True).start()
    for i in range(SIDE):
        final[u, i] = back[i, u]

    ring_step(3)

    for j in range(1, SIDE):
        q2(j, False).wait_recv()
    tokens = dot(place[...], final[...].reshape(1024, HD), TN).astype(BF)
    picked[0] = tokens[:TOK]
    picked[1] = tokens[TOK:]
    ax_send = to_seq(picked.at[oc], routed_out.at[c], ax_s, ax_r, sibling)
    ax_send.start()
    routed_out[c] = picked[c]
    to_seq(picked.at[oc], routed_out.at[oc], ax_s, ax_r, sibling).wait_recv()
    acts[:, 0:HD] = routed_out[0]
    acts[:, HD : 2 * HD] = routed_out[1]

    def send_a(yy):
        head, e = div(yy, 2), rem(yy, 2)
        return to_head(
            stage_a.at[yy], arrived.at[h, e, :, e], xa_s.at[yy],
            xa_r.at[rem(head + GROUPS - h, GROUPS), e], head,
        )

    def send_b(pair, head):
        q, par = div(pair, 2), rem(pair, 2)
        return to_head(
            stage_b.at[pair, head], arrived.at[h, 1 - par, q, par], xb_s.at[pair, head],
            xb_r.at[rem(head + GROUPS - h, GROUPS), pair], jnp.int32(head),
        )

    def project_a(at):
        yy = rem(at + SIDE, SIDE)
        head, e = div(yy, 2), rem(yy, 2)
        rows = jnp.concatenate([wt[head, e, 0, e], wt[head, e, 1, e]], axis=0)
        share = dot(acts[...], rows, NT).astype(BF)
        stage_a[yy, 0] = share[:, :HD]
        stage_a[yy, 1] = share[:, HD:]

        @pl.when(head == h)
        def _():
            arrived[h, e, 0, e] = share[:, :HD]
            arrived[h, e, 1, e] = share[:, HD:]

        @pl.when(head != h)
        def _():
            send_a(yy).start()

    def project_b(at):
        pair = rem(at + 4, 4)
        q, par = div(pair, 2), rem(pair, 2)
        rows = jnp.concatenate([wt[i, 1 - par, q, par] for i in range(4)], axis=0)
        share = dot(acts[...], rows, NT).astype(BF)
        for head in range(GROUPS):
            tile = share[:, head * HD : (head + 1) * HD]
            stage_b[pair, head] = tile

            @pl.when(h == head)
            def _():
                arrived[h, 1 - par, q, par] = tile

            @pl.when(h != head)
            def _():
                send_b(pair, head).start()

    zb, zp = rem(z, 2), div(z, 2)
    turn = 1 - 2 * zb
    sib_wait(0)
    project_a(y)
    sib_wait(1)
    project_b(zp)
    project_a(y - 1)
    project_a(y + 1)
    sib_wait(2)
    project_b(zp - turn + 4)
    project_a(y - 2)
    project_a(y + 2)
    ring_step(4)
    sib_wait(3)
    project_b(zp + turn)
    project_a(y - 3)
    project_a(y + 3)
    ring_step(5)
    sib_wait(4)
    project_b(zp + 2)
    project_a(y + 4)

    for j in range(1, GROUPS):
        src = rem(h + GROUPS - j, GROUPS)
        for e in range(2):
            to_head(
                stage_a.at[0], arrived.at[src, e, :, e], xa_s.at[0], xa_r.at[j, e], src
            ).wait_recv()
        for pair in range(4):
            q, par = pair // 2, pair % 2
            to_head(
                stage_b.at[0, 0], arrived.at[src, 1 - par, q, par], xb_s.at[0, 0], xb_r.at[j, pair], src
            ).wait_recv()
    for e in range(2):
        for q in range(2):
            for par in range(2):
                total = arrived[0, e, q, par].astype(F32)
                for g in range(1, GROUPS):
                    total = total + arrived[g, e, q, par].astype(F32)
                first = e * 512 + (2 * q + par) * HD
                out[:, first : first + HD] = total.astype(BF)

    for copy in a0:
        copy.wait_send()

    @pl.when(s < 2 * SIDE * SIDE - 1)
    def _():
        halo_copy.wait_send()

    @pl.when(jnp.logical_not(holds))
    def _():
        wx_send.wait_send()

    for j in range(1, SIDE):
        for stage in (p1, p2, q1, q2):
            stage(j, True).wait_send()

    def drain(core):
        @pl.when(holds)
        def _():
            for j in range(1, SIDE):
                w1(j, core, True).wait_send()

        for k in range(1, SIDE // 2 + 1):
            for way in range(2):
                ring(k, way, core, True).wait_send()
        for k in range(SIDE // 2 + 1):
            for way in ways(k):
                sib(k, way, core).wait_send()

    by_core(drain)
    ax_send.wait_send()
    for yy in range(SIDE):

        @pl.when(h != yy // 2)
        def _():
            send_a(jnp.int32(yy)).wait_send()

    for head in range(GROUPS):

        @pl.when(h != head)
        def _():
            for pair in range(4):
                send_b(jnp.int32(pair), head).wait_send()


def on_device(routed_qkv, local_qkv, cluster_ids, wo_routed, wo_local):
    cluster = cluster_ids[:, :, 0]
    order = jnp.arange(TOK, dtype=I32)
    same = (cluster[:, :, None] == cluster[:, None, :]) & (order[None, :, None] < order[None, None, :])
    rank = jnp.sum(same.astype(I32), axis=1)
    code = jnp.broadcast_to((cluster * 2 + rank)[:, None, :], (2, 8, TOK))
    sems = [
        (4,), (4,), (), (), (), (), (8,), (8,), (8,), (8,), (8,), (8,),
        (5, 2), (5, 2), (5, 2), (5, 2), (8,), (8,), (8,), (8,), (), (),
        (8,), (4, 2), (4, 4), (4, 4),
    ]
    scratch = [
        pltpu.VMEM((2, TOK, 3 * HD), BF),
        pltpu.VMEM((2, 8, TOK), I32),
        pltpu.VMEM((1024, 2 * TOK), BF),
        pltpu.VMEM((8, 8, 16, 3 * HD), BF),
        pltpu.VMEM((8, 8, 16, 3 * HD), BF),
        pltpu.VMEM((8, 8, 16, 3 * HD), BF),
        pltpu.VMEM((8, 8, 16, HD), BF),
        pltpu.VMEM((8, 8, 16, HD), BF),
        pltpu.VMEM((8, 8, 16, HD), BF),
        pltpu.VMEM((2, TOK, HD), BF),
        pltpu.VMEM((2, TOK, HD), BF),
        pltpu.VMEM((TOK, 8 * HD), BF),
        pltpu.VMEM((2, TOK, LOCAL * HD), BF),
        pltpu.VMEM((32, 8 * HD), BF),
        pltpu.VMEM((4, 2, 2, 2, 128, 8 * HD), BF),
        pltpu.VMEM((8, 2, TOK, HD), BF),
        pltpu.VMEM((4, 4, TOK, HD), BF),
        pltpu.VMEM((4, 2, 2, 2, TOK, HD), BF),
    ]
    scratch += [pltpu.SemaphoreType.DMA(shape) if shape else pltpu.SemaphoreType.DMA for shape in sems]
    return pl.pallas_call(
        kernel,
        out_shape=jax.ShapeDtypeStruct((TOK, 1024), BF),
        in_specs=[pl.BlockSpec(memory_space=pltpu.VMEM)] * 5,
        out_specs=pl.BlockSpec(memory_space=pltpu.VMEM),
        scratch_shapes=scratch,
        compiler_params=pltpu.CompilerParams(
            collective_id=0, has_side_effects=True, vmem_limit_bytes=50 * 2**20
        ),
        cost_estimate=pl.CostEstimate(flops=4 * 10**9, bytes_accessed=3 * 2**20, transcendentals=2 * 10**6),
    )(routed_qkv, local_qkv, code, wo_routed, wo_local)


def solution(mesh):
    placed = (
        P(None, "seq", "head"),
        P(None, "seq", "head"),
        P("head", "seq", None),
        P("head", "seq"),
        P("head", "seq"),
    )
    return jax.shard_map(
        on_device, mesh=mesh, in_specs=placed, out_specs=P("seq", "head"), check_vma=False
    )
```

```python
import functools
import math

import jax
import jax.numpy as jnp
from jax import lax
from jax.experimental import pallas as pl
from jax.experimental.pallas import tpu as pltpu
from jax.sharding import PartitionSpec as P

HD = 128
TOK = 256
LOCAL = 6
SIDE = 8
GROUPS = 4
EMPTY = 128.0
NEVER = -1e30
SCALE = 1.0 / math.sqrt(HD)
BF = jnp.bfloat16
F32 = jnp.float32
I32 = jnp.int32
NT = (((1,), (1,)), ((), ()))
NN = (((1,), (0,)), ((), ()))
TN = (((0,), (0,)), ((), ()))


def dot(a, b, dims):
    return lax.dot_general(a, b, dims, preferred_element_type=F32)


def iota(shape, axis):
    return lax.broadcasted_iota(I32, shape, axis)


def each(low, high, body):
    def step(j, carry):
        body(j)
        return carry

    lax.fori_loop(low, high, step, jnp.int32(0))


def div(a, b):
    return lax.div(a, jnp.int32(b))


def rem(a, b):
    return lax.rem(a, jnp.int32(b))


def kernel(
    routed, local_in, ids, wr, wl, out,
    own_x, own_ids, local, place, sent, via, got, answer, back, final, picked, routed_out, acts, halo,
    wt, stage_a, stage_b, arrived,
    in_s, a0_s, a0_r, halo_s, halo_r, wx_s, wx_r, p1_s, p1_r, p2_s, p2_r, w1_s, w1_r,
    ring_s, ring_r, sib_s, sib_r, q1_s, q1_r, q2_s, q2_r, ax_s, ax_r, xa_s, xa_r, xb_s, xb_r,
):
    h = lax.axis_index("head")
    s = lax.axis_index("seq")
    c = rem(s, 2)
    oc = 1 - c
    chip = div(s, 2)
    z = rem(chip, SIDE)
    y = div(chip, SIDE)
    u = z * oc + y * c
    w = y * oc + z * c
    sibling = s + 1 - 2 * c

    def seq_yz(yy, zz):
        return (yy * SIDE + zz) * 2 + c

    def seq_uw(uu, ww):
        return seq_yz(ww * oc + uu * c, uu * oc + ww * c)

    def to_seq(src, dst, ss, rs, seq):
        return pltpu.make_async_remote_copy(
            src_ref=src, dst_ref=dst, send_sem=ss, recv_sem=rs,
            device_id={"seq": seq}, device_id_type=pl.DeviceIdType.MESH,
        )

    def to_head(src, dst, ss, rs, head):
        return pltpu.make_async_remote_copy(
            src_ref=src, dst_ref=dst, send_sem=ss, recv_sem=rs,
            device_id={"head": head}, device_id_type=pl.DeviceIdType.MESH,
        )

    barrier = pltpu.get_barrier_semaphore()

    def greet(j):
        for target in (seq_uw(rem(u + j, SIDE), w), seq_uw(u, rem(w + j, SIDE))):
            pl.semaphore_signal(barrier, inc=1, device_id={"seq": target}, device_id_type=pl.DeviceIdType.MESH)

    each(1, SIDE, greet)
    pl.semaphore_signal(barrier, inc=1, device_id={"seq": sibling}, device_id_type=pl.DeviceIdType.MESH)
    for j in range(1, GROUPS):
        pl.semaphore_signal(
            barrier, inc=1, device_id={"head": rem(h + j, GROUPS)}, device_id_type=pl.DeviceIdType.MESH
        )

    @pl.when((c == 0) & (s > 0))
    def _():
        pl.semaphore_signal(barrier, inc=1, device_id={"seq": s - 1}, device_id_type=pl.DeviceIdType.MESH)

    pl.semaphore_wait(barrier, 2 * (SIDE - 1) + 1 + GROUPS - 1 + c * (1 - div(s, 2 * SIDE * SIDE - 1)))

    def block_of(yy, zz):
        return wt.at[
            div(yy, 2), rem(yy, 2), div(zz, 4), rem(div(zz, 2), 2),
            pl.ds(pl.multiple_of(rem(zz, 2) * 64, 64), 64),
        ]

    def part_of(core, first, count):
        return wt.at[
            div(y, 2), rem(y, 2), div(z, 4), rem(div(z, 2), 2),
            pl.ds(pl.multiple_of(rem(z, 2) * 64 + core * 32, 32), 32), pl.ds(first, count),
        ]

    def holder(yy, zz):
        return rem(yy + div(zz, 2), 2)

    holds = holder(y, z) == c
    pieces = ((wr, 0, 2 * HD), (wl, 2 * HD, LOCAL * HD))
    w_keep = [
        pltpu.make_async_copy(ref, part_of(c, first, count), in_s.at[i])
        for i, (ref, first, count) in enumerate(pieces)
    ]
    w_send = [
        to_seq(ref, part_of(c, first, count), wx_s.at[i], wx_r.at[i], sibling)
        for i, (ref, first, count) in enumerate(pieces)
    ]
    w_take = [
        to_seq(ref, part_of(oc, first, count), wx_s.at[i], wx_r.at[i], sibling)
        for i, (ref, first, count) in enumerate(pieces)
    ]

    @pl.when(holds)
    def _():
        for copy in w_keep:
            copy.start()

    @pl.when(jnp.logical_not(holds))
    def _():
        for copy in w_send:
            copy.start()

    def head_rows(j, core):
        return routed.at[j, :, pl.ds(pl.multiple_of(core * HD, HD), HD)]

    def a0(core):
        copies = [
            to_seq(head_rows(j, oc), own_x.at[core, :, pl.ds(j * HD, HD)], a0_s.at[j], a0_r.at[j], sibling)
            for j in range(3)
        ]
        return copies + [to_seq(ids.at[oc], own_ids.at[core], a0_s.at[3], a0_r.at[3], sibling)]

    for copy in a0(c):
        copy.start()
    own = [
        pltpu.make_async_copy(head_rows(j, c), own_x.at[c, :, pl.ds(j * HD, HD)], in_s.at[2 + j])
        for j in range(3)
    ]
    own.append(pltpu.make_async_copy(ids.at[c], own_ids.at[c], in_s.at[5]))
    own.append(pltpu.make_async_copy(local_in, local, in_s.at[6]))
    for copy in own:
        copy.start()
    halo_copy = to_seq(local_in.at[pl.ds(1, 2)], halo, halo_s, halo_r, s + 1)
    own_x[:, :, 3 * HD :] = jnp.ones((2, TOK, HD), BF)

    def w1(j, core, sending):
        if core == 0:
            target = seq_yz(y, rem(z + j, SIDE))
            blk = block_of(y, z) if sending else block_of(y, rem(z + SIDE - j, SIDE))
        else:
            target = seq_yz(rem(y + j, SIDE), z)
            blk = block_of(y, z) if sending else block_of(rem(y + SIDE - j, SIDE), z)
        return to_seq(blk, blk, w1_s.at[j], w1_r.at[j], target)

    def by_core(body):
        for core in range(2):
            pl.when(c == core)(functools.partial(body, core))

    @pl.when(holds)
    def _():
        for copy in w_keep:
            copy.wait()
        for copy in w_take:
            copy.wait_recv()

        def send(core):
            each(1, SIDE, lambda j: w1(j, core, True).start())

        by_core(send)

    for copy in own[:4]:
        copy.wait()
    for copy in a0(oc):
        copy.wait_recv()

    def rows_of(b):
        cluster = own_ids[b]
        name = cluster.astype(F32)
        first_row = jnp.where(iota((8, TOK), 0) == 0, jnp.broadcast_to(name, (8, TOK)), 0.0).astype(BF)
        down = dot(first_row, jnp.ones((8, TOK), BF), TN)
        earlier = (down == name) & (iota((TOK, TOK), 0) < iota((TOK, TOK), 1))
        rank = jnp.sum(jnp.where(earlier, 1.0, 0.0), axis=0, keepdims=True).astype(I32)
        owner = cluster >> 2
        turned = (owner & 7) * SIDE + (owner >> 3)
        goes = turned * oc + owner * c
        return goes * 16 + b * 8 + (cluster & 3) * 2 + rank

    slot = jnp.concatenate([rows_of(0), rows_of(1)], axis=1)
    both = own_x[...].reshape(2 * TOK, 4 * HD)

    def fill(i):
        hot = (iota((256, 2 * TOK), 0) + i * 256 == slot).astype(F32).astype(BF)
        place[pl.ds(pl.multiple_of(i * 256, 256), 256)] = hot
        rows = dot(hot, both, NN)
        lead = (1.0 - rows[:, 3 * HD :]) * EMPTY
        rows = jnp.concatenate([rows[:, :HD], rows[:, HD : 2 * HD] + lead, rows[:, 2 * HD : 3 * HD]], axis=1)
        sent[pl.ds(2 * i, 2)] = rows.astype(BF).reshape(2, SIDE, 16, 3 * HD)

    each(0, 4, fill)

    def p1(j, sending):
        there, here = rem(u + j, SIDE), rem(u + SIDE - j, SIDE)
        dst = via.at[u] if sending else via.at[here]
        return to_seq(sent.at[there], dst, p1_s.at[j], p1_r.at[j], seq_uw(there, w))

    each(1, SIDE, lambda j: p1(j, True).start())
    via[u] = sent[u]

    @pl.when(s < 2 * SIDE * SIDE - 1)
    def _():
        halo_copy.start()

    for core in range(2):

        @pl.when(c == core)
        def _():
            def take(j):
                if core == 0:
                    is_source = holder(y, rem(z + SIDE - j, SIDE)) == 0
                else:
                    is_source = holder(rem(y + SIDE - j, SIDE), z) == 1

                @pl.when(is_source)
                def _():
                    w1(j, core, False).wait_recv()

            each(1, SIDE, take)

    def blocks(core, place_on):
        at = rem(place_on + SIDE, SIDE)
        if core == 0:
            return wt.at[div(at, 2), rem(at, 2), :, rem(at, 2)]
        par = rem(div(at, 2), 2)
        return wt.at[:, 1 - par, div(at, 4), par, pl.ds(pl.multiple_of(rem(at, 2) * 64, 64), 64)]

    def half(ref, k, way):
        return ref.at[:, :, pl.ds(way * 512, 512)] if k == SIDE // 2 else ref

    def ring(k, way, core, sending):
        coord = y if core == 0 else z
        sign = 1 - 2 * way
        if sending:
            blk = blocks(core, coord - sign * (k - 1))
        else:
            blk = blocks(core, coord - sign * k)
        blk = half(blk, k, way)
        to = rem(coord + sign + SIDE, SIDE)
        target = seq_yz(to, z) if core == 0 else seq_yz(y, to)
        return to_seq(blk, blk, ring_s.at[k, way], ring_r.at[k, way], target)

    def sib(k, way, path):
        coord = y if path == 0 else z
        blk = blocks(path, coord - (1 - 2 * way) * k)
        return to_seq(blk, blk, sib_s.at[k, way], sib_r.at[k, way], sibling)

    def ways(k):
        return (0,) if k in (0, SIDE // 2) else (0, 1)

    def ring_step(k):
        def body(core):
            if k > 1:
                for way in range(2):
                    ring(k - 1, way, core, False).wait_recv()
            if k <= SIDE // 2:
                for way in range(2):
                    ring(k, way, core, True).start()
            for way in ways(k - 1):
                sib(k - 1, way, core).start()

        by_core(body)

    def sib_wait(k):
        def body(core):
            for way in ways(k):
                sib(k, way, 1 - core).wait_recv()

        by_core(body)

    ring_step(1)

    each(1, SIDE, lambda j: p1(j, False).wait_recv())

    def p2(j, sending, core):
        there, here = rem(w + j, SIDE), rem(w + SIDE - j, SIDE)
        at = w if sending else here
        dst = got.at[at] if core == 0 else got.at[:, at]
        return to_seq(via.at[:, there], dst, p2_s.at[j], p2_r.at[j], seq_uw(u, there))

    def p2_start(core):
        each(1, SIDE, lambda j: p2(j, True, core).start())

        def keep(i):
            if core == 0:
                got[w, i] = via[i, w]
            else:
                got[i, w] = via[i, w]

        each(0, SIDE, keep)

    by_core(p2_start)

    own[4].wait()

    @pl.when(s > 0)
    def _():
        halo_copy.wait_recv()

    @pl.when(s == 0)
    def _():
        halo[...] = jnp.zeros_like(halo)

    own_side = iota((TOK, TOK), 1) <= iota((TOK, TOK), 0)
    shift = jnp.where(s > 0, jnp.float32(0.0), jnp.float32(NEVER))

    def window(n):
        cols = pl.ds(pl.multiple_of(n * HD, HD), HD)
        query = local[0, :, cols]
        here = dot(query, local[1, :, cols], NT) * SCALE
        before = dot(query, halo[0, :, cols], NT) * SCALE + shift
        scores = jnp.where(own_side, here, before)
        raised = jnp.exp(scores - jnp.max(scores, axis=1, keepdims=True))
        weights = raised * (1.0 / jnp.sum(raised, axis=1, keepdims=True))
        near = jnp.where(own_side, weights, 0.0).astype(BF)
        far = jnp.where(own_side, 0.0, weights).astype(BF)
        result = dot(near, local[2, :, cols], NN) + dot(far, halo[1, :, cols], NN)
        acts[:, pl.ds(pl.multiple_of((2 + n) * HD, HD), HD)] = result.astype(BF)

    each(0, LOCAL, window)

    ring_step(2)

    def p2_take(core):
        each(1, SIDE, lambda j: p2(j, False, core).wait_recv())

    by_core(p2_take)

    def code_of(r):
        return ((r >> 1) & 3) * 4096 + (r >> 4) * 4 + ((r >> 3) & 1) * 2 + (r & 1)

    keys = got[:, :, :, HD : 2 * HD].reshape(1024, HD)
    lane_zero = (iota((8, HD), 1) == 0).astype(F32).astype(BF)
    lead_key = dot(lane_zero, keys, NT)[0:1]
    key_code = jnp.where(lead_key < 0.75 * EMPTY, code_of(iota((8, 1024), 1))[0:1], 1 << 20)

    def cluster_rows(last, i):
        keys = got[: last // 128, :, :, HD : 2 * HD].reshape(last, HD)
        values = got[: last // 128, :, :, 2 * HD :].reshape(last, HD)
        query = got[pl.ds(2 * i, 2), :, :, 0:HD].reshape(256, HD)
        scores = dot(query, keys, NT) * SCALE
        ahead = code_of(iota((256, HD), 0) + i * 256)[:, 0:1] - key_code[:, :last]
        scores = jnp.where((ahead >= 0) & (ahead < 256), scores, NEVER)
        raised = jnp.exp(scores - jnp.max(scores, axis=1, keepdims=True))
        weights = (raised * (1.0 / jnp.sum(raised, axis=1, keepdims=True))).astype(BF)
        answer[pl.ds(2 * i, 2)] = dot(weights, values, NN).astype(BF).reshape(2, SIDE, 16, HD)

    each(0, 2, functools.partial(cluster_rows, 512))
    each(2, 4, functools.partial(cluster_rows, 1024))

    def q1(j, sending, core):
        there, here = rem(w + j, SIDE), rem(w + SIDE - j, SIDE)
        src = answer.at[there] if core == 0 else answer.at[:, there]
        dst = back.at[w] if sending else back.at[here]
        return to_seq(src, dst, q1_s.at[j], q1_r.at[j], seq_uw(u, there))

    def q1_start(core):
        each(1, SIDE, lambda j: q1(j, True, core).start())

        def keep(i):
            back[w, i] = answer[w, i] if core == 0 else answer[i, w]

        each(0, SIDE, keep)

    by_core(q1_start)


    each(1, SIDE, lambda j: q1(j, False, 0).wait_recv())

    def q2(j, sending):
        there, here = rem(u + j, SIDE), rem(u + SIDE - j, SIDE)
        dst = final.at[u] if sending else final.at[here]
        return to_seq(back.at[:, there], dst, q2_s.at[j], q2_r.at[j], seq_uw(there, w))

    each(1, SIDE, lambda j: q2(j, True).start())

    def keep_final(i):
        final[u, i] = back[i, u]

    each(0, SIDE, keep_final)

    ring_step(3)

    each(1, SIDE, lambda j: q2(j, False).wait_recv())
    tokens = dot(place[...], final[...].reshape(1024, HD), TN).astype(BF)
    picked[0] = tokens[:TOK]
    picked[1] = tokens[TOK:]
    ax_send = to_seq(picked.at[oc], routed_out.at[c], ax_s, ax_r, sibling)
    ax_send.start()
    routed_out[c] = picked[c]
    to_seq(picked.at[oc], routed_out.at[oc], ax_s, ax_r, sibling).wait_recv()
    acts[:, 0:HD] = routed_out[0]
    acts[:, HD : 2 * HD] = routed_out[1]

    def send_a(yy):
        head, e = div(yy, 2), rem(yy, 2)
        return to_head(
            stage_a.at[yy], arrived.at[h, e, :, e], xa_s.at[yy],
            xa_r.at[rem(head + GROUPS - h, GROUPS), e], head,
        )

    def send_b(pair, head):
        q, par = div(pair, 2), rem(pair, 2)
        return to_head(
            stage_b.at[pair, head], arrived.at[h, 1 - par, q, par], xb_s.at[pair, head],
            xb_r.at[rem(head + GROUPS - h, GROUPS), pair], jnp.int32(head),
        )

    def project_a(at):
        yy = rem(at + SIDE, SIDE)
        head, e = div(yy, 2), rem(yy, 2)
        rows = jnp.concatenate([wt[head, e, 0, e], wt[head, e, 1, e]], axis=0)
        share = dot(acts[...], rows, NT).astype(BF)
        stage_a[yy, 0] = share[:, :HD]
        stage_a[yy, 1] = share[:, HD:]

        @pl.when(head == h)
        def _():
            arrived[h, e, 0, e] = share[:, :HD]
            arrived[h, e, 1, e] = share[:, HD:]

        @pl.when(head != h)
        def _():
            send_a(yy).start()

    def project_b(at):
        pair = rem(at + 4, 4)
        q, par = div(pair, 2), rem(pair, 2)
        rows = jnp.concatenate([wt[i, 1 - par, q, par] for i in range(4)], axis=0)
        share = dot(acts[...], rows, NT).astype(BF)
        for head in range(GROUPS):
            tile = share[:, head * HD : (head + 1) * HD]
            stage_b[pair, head] = tile

            @pl.when(h == head)
            def _():
                arrived[h, 1 - par, q, par] = tile

            @pl.when(h != head)
            def _():
                send_b(pair, head).start()

    zb, zp = rem(z, 2), div(z, 2)
    turn = 1 - 2 * zb

    def swing(t):
        return div(t + 1, 2) * (1 - 2 * rem(t, 2))

    def share_out(k):
        for step in range(SIDE // 2 + 1):

            @pl.when(k == step)
            def _():
                if step >= 3:
                    ring_step(step + 1)
                sib_wait(step)

        @pl.when(k > 0)
        def _():
            project_b(zp + turn * swing(k - 1) + 4)

        each(jnp.maximum(2 * k - 1, 0), jnp.minimum(2 * k + 1, SIDE), lambda t: project_a(y + swing(t)))

    each(0, SIDE // 2 + 1, share_out)

    for j in range(1, GROUPS):
        src = rem(h + GROUPS - j, GROUPS)
        for e in range(2):
            to_head(
                stage_a.at[0], arrived.at[src, e, :, e], xa_s.at[0], xa_r.at[j, e], src
            ).wait_recv()
        for pair in range(4):
            q, par = pair // 2, pair % 2
            to_head(
                stage_b.at[0, 0], arrived.at[src, 1 - par, q, par], xb_s.at[0, 0], xb_r.at[j, pair], src
            ).wait_recv()

    def add_up(n):
        e, q, par = div(n, 4), rem(div(n, 2), 2), rem(n, 2)
        total = arrived[0, e, q, par].astype(F32)
        for g in range(1, GROUPS):
            total = total + arrived[g, e, q, par].astype(F32)
        out[:, pl.ds(pl.multiple_of(n * HD, HD), HD)] = total.astype(BF)

    each(0, 8, add_up)

    for copy in a0(c):
        copy.wait_send()

    @pl.when(s < 2 * SIDE * SIDE - 1)
    def _():
        halo_copy.wait_send()

    @pl.when(jnp.logical_not(holds))
    def _():
        for copy in w_send:
            copy.wait_send()

    def left(j):
        p1(j, True).wait_send()
        q2(j, True).wait_send()

    each(1, SIDE, left)

    def drain(core):
        def left(j):
            p2(j, True, core).wait_send()
            q1(j, True, core).wait_send()

        each(1, SIDE, left)

        @pl.when(holds)
        def _():
            each(1, SIDE, lambda j: w1(j, core, True).wait_send())

        for k in range(1, SIDE // 2 + 1):
            for way in range(2):
                ring(k, way, core, True).wait_send()
        for k in range(SIDE // 2 + 1):
            for way in ways(k):
                sib(k, way, core).wait_send()

    by_core(drain)
    ax_send.wait_send()
    def left_a(yy):
        @pl.when(h != div(yy, 2))
        def _():
            send_a(yy).wait_send()

    each(0, SIDE, left_a)

    for head in range(GROUPS):

        @pl.when(h != head)
        def _():
            each(0, 4, lambda pair: send_b(pair, head).wait_send())


def on_device(routed_qkv, local_qkv, cluster_ids, wo_routed, wo_local):
    sems = [
        (7,), (4,), (4,), (), (), (2,), (2,), (8,), (8,), (8,), (8,), (8,), (8,),
        (5, 2), (5, 2), (5, 2), (5, 2), (8,), (8,), (8,), (8,), (), (),
        (8,), (4, 2), (4, 4), (4, 4),
    ]
    scratch = [
        pltpu.VMEM((2, TOK, 4 * HD), BF),
        pltpu.VMEM((2, 1, TOK), I32),
        pltpu.VMEM((3, TOK, LOCAL * HD), BF),
        pltpu.VMEM((1024, 2 * TOK), BF),
        pltpu.VMEM((8, 8, 16, 3 * HD), BF),
        pltpu.VMEM((8, 8, 16, 3 * HD), BF),
        pltpu.VMEM((8, 8, 16, 3 * HD), BF),
        pltpu.VMEM((8, 8, 16, HD), BF),
        pltpu.VMEM((8, 8, 16, HD), BF),
        pltpu.VMEM((8, 8, 16, HD), BF),
        pltpu.VMEM((2, TOK, HD), BF),
        pltpu.VMEM((2, TOK, HD), BF),
        pltpu.VMEM((TOK, 8 * HD), BF),
        pltpu.VMEM((2, TOK, LOCAL * HD), BF),
        pltpu.VMEM((4, 2, 2, 2, 128, 8 * HD), BF),
        pltpu.VMEM((8, 2, TOK, HD), BF),
        pltpu.VMEM((4, 4, TOK, HD), BF),
        pltpu.VMEM((4, 2, 2, 2, TOK, HD), BF),
    ]
    scratch += [pltpu.SemaphoreType.DMA(shape) if shape else pltpu.SemaphoreType.DMA for shape in sems]
    return pl.pallas_call(
        kernel,
        out_shape=jax.ShapeDtypeStruct((TOK, 1024), BF),
        in_specs=[pl.BlockSpec(memory_space=pltpu.HBM)] * 5,
        out_specs=pl.BlockSpec(memory_space=pltpu.VMEM),
        scratch_shapes=scratch,
        compiler_params=pltpu.CompilerParams(
            collective_id=0, has_side_effects=True, vmem_limit_bytes=60 * 2**20
        ),
        cost_estimate=pl.CostEstimate(flops=4 * 10**9, bytes_accessed=3 * 2**20, transcendentals=2 * 10**6),
    )(routed_qkv, local_qkv, cluster_ids.transpose(0, 2, 1), wo_routed.T, wo_local.T)


def solution(mesh):
    placed = (
        P(None, "seq", "head"),
        P(None, "seq", "head"),
        P("head", "seq", None),
        P("head", "seq"),
        P("head", "seq"),
    )
    return jax.shard_map(
        on_device, mesh=mesh, in_specs=placed, out_specs=P("seq", "head"), check_vma=False
    )
```

```python
import functools
import math

import jax
import jax.numpy as jnp
from jax import lax
from jax.experimental import pallas as pl
from jax.experimental.pallas import tpu as pltpu
from jax.sharding import PartitionSpec as P

HD = 128
TOK = 256
LOCAL = 6
SIDE = 8
GROUPS = 4
EMPTY = 128.0
NEVER = -1e30
SCALE = 1.0 / math.sqrt(HD)
BF = jnp.bfloat16
F32 = jnp.float32
I32 = jnp.int32
NT = (((1,), (1,)), ((), ()))
NN = (((1,), (0,)), ((), ()))
TN = (((0,), (0,)), ((), ()))


def dot(a, b, dims):
    return lax.dot_general(a, b, dims, preferred_element_type=F32)


def iota(shape, axis):
    return lax.broadcasted_iota(I32, shape, axis)


def each(low, high, body):
    for j in range(low, high):
        body(j)


def div(a, b):
    if isinstance(a, int):
        return a // b
    return lax.div(a, jnp.int32(b))


def rem(a, b):
    if isinstance(a, int):
        return a % b
    return lax.rem(a, jnp.int32(b))


def kernel(
    routed, local_in, ids, wr, wl, out,
    own_x, own_ids, local, place, sent, via, got, answer, back, final, picked, acts, routed_acts, halo,
    wt, summed,
    in_s, a0_s, a0_r, halo_s, halo_r, wx_s, wx_r, p1_s, p1_r, p2_s, p2_r, w1_s, w1_r,
    ring_s, ring_r, sib_s, sib_r, q1_s, q1_r, q2_s, q2_r, xl_s, xl_r, xr_s, xr_r,
):
    h = lax.axis_index("head")
    s = lax.axis_index("seq")
    c = rem(s, 2)
    oc = 1 - c
    chip = div(s, 2)
    z = rem(chip, SIDE)
    y = div(chip, SIDE)
    u = z * oc + y * c
    w = y * oc + z * c
    sibling = s + 1 - 2 * c

    def seq_yz(yy, zz):
        return (yy * SIDE + zz) * 2 + c

    def seq_uw(uu, ww):
        return seq_yz(ww * oc + uu * c, uu * oc + ww * c)

    def to_seq(src, dst, ss, rs, seq):
        return pltpu.make_async_remote_copy(
            src_ref=src, dst_ref=dst, send_sem=ss, recv_sem=rs,
            device_id={"seq": seq}, device_id_type=pl.DeviceIdType.MESH,
        )

    def to_any(src, dst, ss, rs, seq, head):
        return pltpu.make_async_remote_copy(
            src_ref=src, dst_ref=dst, send_sem=ss, recv_sem=rs,
            device_id={"seq": seq, "head": head}, device_id_type=pl.DeviceIdType.MESH,
        )

    def hello(seq, head):
        pl.semaphore_signal(
            barrier, inc=1, device_id={"seq": seq, "head": head}, device_id_type=pl.DeviceIdType.MESH
        )

    def w_target(r):
        return div(y, 2), rem(y, 2) * 4 + c * 2 + r, div(h, 2)

    def w_source(i):
        return 2 * c + i, 2 * h + div(y, 4), div(rem(y, 4), 2)

    def target_is_me(r):
        head, row, core = w_target(r)
        return (head == h) & (row == y) & (core == c)

    def source_is_me(i):
        head, row, core = w_source(i)
        return (head == h) & (row == y) & (core == c)

    barrier = pltpu.get_barrier_semaphore()

    def greet(j):
        for target in (seq_uw(rem(u + j, SIDE), w), seq_uw(u, rem(w + j, SIDE))):
            pl.semaphore_signal(barrier, inc=1, device_id={"seq": target}, device_id_type=pl.DeviceIdType.MESH)

    each(1, SIDE, greet)
    pl.semaphore_signal(barrier, inc=1, device_id={"seq": sibling}, device_id_type=pl.DeviceIdType.MESH)
    for j in range(1, GROUPS):
        hello(s, rem(h + j, GROUPS))
        hello(sibling, rem(h + j, GROUPS))
    for i in range(2):
        head, row, core = w_source(i)

        @pl.when(jnp.logical_not(source_is_me(i)))
        def _():
            hello((row * SIDE + z) * 2 + core, head)

    @pl.when((c == 0) & (s > 0))
    def _():
        pl.semaphore_signal(barrier, inc=1, device_id={"seq": s - 1}, device_id_type=pl.DeviceIdType.MESH)

    selves = jnp.where(target_is_me(0) | target_is_me(1), 1, 0)
    expected = 2 * (SIDE - 1) + 1 + 2 * (GROUPS - 1) + 2
    pl.semaphore_wait(barrier, expected + c * (1 - div(s, 2 * SIDE * SIDE - 1)) - selves)

    def lanes(first, count):
        return pl.ds(pl.multiple_of(first, HD), count)

    pieces = ((wr, 0, 2 * HD), (wl, 4 * HD, LOCAL * HD))

    def w_landing(row, head, piece):
        _, first, count = pieces[piece]
        at = lanes(div(head, 2) * 16 * HD + first + rem(head, 2) * count, count)
        return wt.at[div(row, 4), z, rem(row, 4), :, at]

    def w_send(r, piece):
        head, row, core = w_target(r)
        src = pieces[piece][0].at[pl.ds(r * 16, 16)]
        return to_any(
            src, w_landing(row, h, piece), wx_s.at[r, piece], wx_r.at[rem(h, 2), piece],
            (row * SIDE + z) * 2 + core, head,
        )

    def w_keep(r, piece):
        src = pieces[piece][0].at[pl.ds(r * 16, 16)]
        return pltpu.make_async_copy(src, w_landing(w_target(r)[1], h, piece), in_s.at[piece])

    def w_take(i, piece):
        head, row, core = w_source(i)
        src = pieces[piece][0].at[pl.ds(0, 16)]
        return to_any(
            src, w_landing(y, head, piece), wx_s.at[0, piece], wx_r.at[i, piece],
            (row * SIDE + z) * 2 + core, head,
        )

    for r in range(2):
        me = target_is_me(r)

        @pl.when(me)
        def _():
            for piece in range(2):
                w_keep(r, piece).start()

        @pl.when(jnp.logical_not(me))
        def _():
            for piece in range(2):
                w_send(r, piece).start()

    def head_rows(j, core):
        return routed.at[j, :, pl.ds(pl.multiple_of(core * HD, HD), HD)]

    def a0(core):
        copies = [
            to_seq(head_rows(j, oc), own_x.at[core, :, pl.ds(j * HD, HD)], a0_s.at[j], a0_r.at[j], sibling)
            for j in range(3)
        ]
        return copies + [to_seq(ids.at[oc], own_ids.at[core], a0_s.at[3], a0_r.at[3], sibling)]

    for copy in a0(c):
        copy.start()
    own = [
        pltpu.make_async_copy(head_rows(j, c), own_x.at[c, :, pl.ds(j * HD, HD)], in_s.at[2 + j])
        for j in range(3)
    ]
    own.append(pltpu.make_async_copy(ids.at[c], own_ids.at[c], in_s.at[5]))
    own.append(pltpu.make_async_copy(local_in, local, in_s.at[6]))
    for copy in own:
        copy.start()
    halo_copy = to_seq(local_in.at[pl.ds(1, 2)], halo, halo_s, halo_r, s + 1)
    own_x[:, :, 3 * HD :] = jnp.ones((2, TOK, HD), BF)

    def block_of(core, yy, zz):
        return wt.at[div(yy, 4), zz, rem(yy, 4), :, pl.ds(core * 16 * HD, 16 * HD)]

    def w1(j, core, sending):
        if core == 0:
            target = seq_yz(y, rem(z + j, SIDE))
            here = rem(z + SIDE - j, SIDE)
            blk = block_of(core, y, z) if sending else block_of(core, y, here)
        else:
            target = seq_yz(rem(y + j, SIDE), z)
            here = rem(y + SIDE - j, SIDE)
            blk = block_of(core, y, z) if sending else block_of(core, here, z)
        return to_seq(blk, blk, w1_s.at[j], w1_r.at[j], target)

    def by_core(body):
        for core in range(2):
            pl.when(c == core)(functools.partial(body, core))

    for copy in own[:4]:
        copy.wait()
    for copy in a0(oc):
        copy.wait_recv()

    def rows_of(b):
        cluster = own_ids[b]
        name = cluster.astype(F32)
        first_row = jnp.where(iota((8, TOK), 0) == 0, jnp.broadcast_to(name, (8, TOK)), 0.0).astype(BF)
        down = dot(first_row, jnp.ones((8, TOK), BF), TN)
        earlier = (down == name) & (iota((TOK, TOK), 0) < iota((TOK, TOK), 1))
        rank = jnp.sum(jnp.where(earlier, 1.0, 0.0), axis=0, keepdims=True).astype(I32)
        owner = cluster >> 2
        turned = (owner & 7) * SIDE + (owner >> 3)
        goes = turned * oc + owner * c
        return goes * 16 + b * 8 + (cluster & 3) * 2 + rank

    slot = jnp.concatenate([rows_of(0), rows_of(1)], axis=1)
    both = own_x[...].reshape(2 * TOK, 4 * HD)

    def fill(i):
        hot = (iota((256, 2 * TOK), 0) + i * 256 == slot).astype(F32).astype(BF)
        place[pl.ds(i * 256, 256)] = hot
        rows = dot(hot, both, NN)
        lead = (1.0 - rows[:, 3 * HD :]) * EMPTY
        rows = jnp.concatenate([rows[:, :HD], rows[:, HD : 2 * HD] + lead, rows[:, 2 * HD : 3 * HD]], axis=1)
        sent[pl.ds(2 * i, 2)] = rows.astype(BF).reshape(2, SIDE, 16, 3 * HD)

    each(0, 4, fill)

    def p1(j, sending):
        there, here = rem(u + j, SIDE), rem(u + SIDE - j, SIDE)
        dst = via.at[u] if sending else via.at[here]
        return to_seq(sent.at[there], dst, p1_s.at[j], p1_r.at[j], seq_uw(there, w))

    each(1, SIDE, lambda j: p1(j, True).start())
    via[u] = sent[u]

    for i in range(2):
        me = source_is_me(i)
        for piece in range(2):

            @pl.when(me)
            def _():
                r = rem(y, 2)
                for value in range(2):

                    @pl.when(r == value)
                    def _():
                        w_keep(value, piece).wait()

            @pl.when(jnp.logical_not(me))
            def _():
                w_take(i, piece).wait_recv()

    def w1_start(core):
        each(1, SIDE, lambda j: w1(j, core, True).start())

    by_core(w1_start)

    @pl.when(s < 2 * SIDE * SIDE - 1)
    def _():
        halo_copy.start()

    def w1_take(core):
        each(1, SIDE, lambda j: w1(j, core, False).wait_recv())

    by_core(w1_take)

    def blocks(core, place_on, first=0, count=16 * HD):
        at = rem(place_on + SIDE, SIDE)
        part = pl.ds(core * 16 * HD + first, count)
        if core == 0:
            return wt.at[div(at, 4), :, rem(at, 4), :, part]
        return wt.at[:, at, :, :, part]

    def ring(k, way, core, sending):
        coord = y if core == 0 else z
        sign = 1 - 2 * way
        if sending:
            at = coord - sign * (k - 1)
        else:
            at = coord - sign * k
        blk = blocks(core, at, way * 8 * HD, 8 * HD) if k == SIDE // 2 else blocks(core, at)
        to = rem(coord + sign + SIDE, SIDE)
        target = seq_yz(to, z) if core == 0 else seq_yz(y, to)
        return to_seq(blk, blk, ring_s.at[k, way], ring_r.at[k, way], target)

    def sib(k, way, path):
        coord = y if path == 0 else z
        blk = blocks(path, coord - (1 - 2 * way) * k)
        return to_seq(blk, blk, sib_s.at[k, way], sib_r.at[k, way], sibling)

    def ways(k):
        return (0,) if k in (0, SIDE // 2) else (0, 1)

    def ring_step(k):
        def body(core):
            if k > 1:
                for way in range(2):
                    ring(k - 1, way, core, False).wait_recv()
            if k <= SIDE // 2:
                for way in range(2):
                    ring(k, way, core, True).start()
            for way in ways(k - 1):
                sib(k - 1, way, core).start()

        by_core(body)

    def sib_wait(k):
        def body(core):
            for way in ways(k):
                sib(k, way, 1 - core).wait_recv()

        by_core(body)

    ring_step(1)

    each(1, SIDE, lambda j: p1(j, False).wait_recv())

    def p2(j, sending, core):
        there, here = rem(w + j, SIDE), rem(w + SIDE - j, SIDE)
        at = w if sending else here
        dst = got.at[at] if core == 0 else got.at[:, at]
        return to_seq(via.at[:, there], dst, p2_s.at[j], p2_r.at[j], seq_uw(u, there))

    def p2_start(core):
        each(1, SIDE, lambda j: p2(j, True, core).start())

        def keep(i):
            if core == 0:
                got[w, i] = via[i, w]
            else:
                got[i, w] = via[i, w]

        each(0, SIDE, keep)

    by_core(p2_start)

    own[4].wait()

    @pl.when(s > 0)
    def _():
        halo_copy.wait_recv()

    @pl.when(s == 0)
    def _():
        halo[...] = jnp.zeros_like(halo)

    own_side = iota((TOK, TOK), 1) <= iota((TOK, TOK), 0)
    shift = jnp.where(s > 0, jnp.float32(0.0), jnp.float32(NEVER))

    def window(n):
        cols = pl.ds(n * HD, HD)
        query = local[0, :, cols]
        here = dot(query, local[1, :, cols], NT) * SCALE
        before = dot(query, halo[0, :, cols], NT) * SCALE + shift
        scores = jnp.where(own_side, here, before)
        raised = jnp.exp(scores - jnp.max(scores, axis=1, keepdims=True))
        weights = raised * (1.0 / jnp.sum(raised, axis=1, keepdims=True))
        near = jnp.where(own_side, weights, 0.0).astype(BF)
        far = jnp.where(own_side, 0.0, weights).astype(BF)
        result = dot(near, local[2, :, cols], NN) + dot(far, halo[1, :, cols], NN)
        acts[h, :, pl.ds(n * HD, HD)] = result.astype(BF)

    each(0, LOCAL, window)

    def xl(j, sending):
        there, here = rem(h + j, GROUPS), rem(h + GROUPS - j, GROUPS)
        dst = acts.at[h] if sending else acts.at[here]
        return to_any(acts.at[h], dst, xl_s.at[j], xl_r.at[j], s, there)

    each(1, GROUPS, lambda j: xl(j, True).start())

    ring_step(2)

    def p2_take(core):
        each(1, SIDE, lambda j: p2(j, False, core).wait_recv())

    by_core(p2_take)

    def code_of(r):
        return ((r >> 1) & 3) * 4096 + (r >> 4) * 4 + ((r >> 3) & 1) * 2 + (r & 1)

    keys = got[:, :, :, HD : 2 * HD].reshape(1024, HD)
    lane_zero = (iota((8, HD), 1) == 0).astype(F32).astype(BF)
    lead_key = dot(lane_zero, keys, NT)[0:1]
    key_code = jnp.where(lead_key < 0.75 * EMPTY, code_of(iota((8, 1024), 1))[0:1], 1 << 20)

    def cluster_rows(last, i):
        keys = got[: last // 128, :, :, HD : 2 * HD].reshape(last, HD)
        values = got[: last // 128, :, :, 2 * HD :].reshape(last, HD)
        query = got[pl.ds(2 * i, 2), :, :, 0:HD].reshape(256, HD)
        scores = dot(query, keys, NT) * SCALE
        ahead = code_of(iota((256, HD), 0) + i * 256)[:, 0:1] - key_code[:, :last]
        scores = jnp.where((ahead >= 0) & (ahead < 256), scores, NEVER)
        raised = jnp.exp(scores - jnp.max(scores, axis=1, keepdims=True))
        weights = (raised * (1.0 / jnp.sum(raised, axis=1, keepdims=True))).astype(BF)
        answer[pl.ds(2 * i, 2)] = dot(weights, values, NN).astype(BF).reshape(2, SIDE, 16, HD)

    for i in range(4):
        cluster_rows((i + 1) * 256, i)

    def q1(j, sending, core):
        there, here = rem(w + j, SIDE), rem(w + SIDE - j, SIDE)
        src = answer.at[there] if core == 0 else answer.at[:, there]
        dst = back.at[w] if sending else back.at[here]
        return to_seq(src, dst, q1_s.at[j], q1_r.at[j], seq_uw(u, there))

    def q1_start(core):
        each(1, SIDE, lambda j: q1(j, True, core).start())

        def keep(i):
            back[w, i] = answer[w, i] if core == 0 else answer[i, w]

        each(0, SIDE, keep)

    by_core(q1_start)


    ring_step(3)

    each(1, SIDE, lambda j: q1(j, False, 0).wait_recv())

    def q2(j, sending):
        there, here = rem(u + j, SIDE), rem(u + SIDE - j, SIDE)
        dst = final.at[u] if sending else final.at[here]
        return to_seq(back.at[:, there], dst, q2_s.at[j], q2_r.at[j], seq_uw(there, w))

    each(1, SIDE, lambda j: q2(j, True).start())

    def keep_final(i):
        final[u, i] = back[i, u]

    each(0, SIDE, keep_final)

    ring_step(4)

    each(1, SIDE, lambda j: q2(j, False).wait_recv())
    tokens = dot(place[...], final[...].reshape(1024, HD), TN).astype(BF)
    picked[0] = tokens[:TOK]
    picked[1] = tokens[TOK:]

    def xr(j, b, sending):
        there, here = rem(h + j, GROUPS), rem(h + GROUPS - j, GROUPS)
        own_side = c * (1 - b) + oc * b
        to = s * (1 - b) + sibling * b
        if sending:
            src, dst = picked.at[own_side], routed_acts.at[h, c]
        else:
            src, dst = picked.at[0], routed_acts.at[here, own_side]
        return to_any(src, dst, xr_s.at[j, b], xr_r.at[j, b], to, there if sending else here)

    for j in range(GROUPS):
        for b in range(2):
            if j or b:
                xr(j, b, True).start()
    routed_acts[h, c] = picked[c]

    ring_step(5)
    for k in range(SIDE // 2 + 1):
        sib_wait(k)
    each(1, GROUPS, lambda j: xl(j, False).wait_recv())

    def rows_at(first, count):
        return wt[:, :, :, :, first : first + count].reshape(1024, count)

    total = jnp.zeros((TOK, 1024), F32)
    for g in range(GROUPS):
        total = total + dot(acts[g], rows_at(g // 2 * 16 * HD + (4 + g % 2 * LOCAL) * HD, LOCAL * HD), NT)
    summed[...] = total
    for j in range(GROUPS):
        for b in range(2):
            if j or b:
                xr(j, b, False).wait_recv()
    total = summed[...]
    for half in range(2):
        wide = jnp.concatenate([routed_acts[2 * half + g, n] for g in range(2) for n in range(2)], axis=1)
        total = total + dot(wide, rows_at(half * 16 * HD, 4 * HD), NT)
    out[...] = total.astype(BF)

    for copy in a0(c):
        copy.wait_send()

    @pl.when(s < 2 * SIDE * SIDE - 1)
    def _():
        halo_copy.wait_send()

    for r in range(2):

        @pl.when(jnp.logical_not(target_is_me(r)))
        def _():
            for piece in range(2):
                w_send(r, piece).wait_send()

    def left(j):
        p1(j, True).wait_send()
        q2(j, True).wait_send()

    each(1, SIDE, left)

    def drain(core):
        def left(j):
            p2(j, True, core).wait_send()
            q1(j, True, core).wait_send()

        each(1, SIDE, left)

        each(1, SIDE, lambda j: w1(j, core, True).wait_send())

        for k in range(1, SIDE // 2 + 1):
            for way in range(2):
                ring(k, way, core, True).wait_send()
        for k in range(SIDE // 2 + 1):
            for way in ways(k):
                sib(k, way, core).wait_send()

    by_core(drain)
    each(1, GROUPS, lambda j: xl(j, True).wait_send())
    for j in range(GROUPS):
        for b in range(2):
            if j or b:
                xr(j, b, True).wait_send()


def on_device(routed_qkv, local_qkv, cluster_ids, wo_routed, wo_local):
    sems = [
        (7,), (4,), (4,), (), (), (2, 2), (2, 2), (8,), (8,), (8,), (8,), (8,), (8,),
        (5, 2), (5, 2), (5, 2), (5, 2), (8,), (8,), (8,), (8,),
        (4,), (4,), (4, 2), (4, 2),
    ]
    scratch = [
        pltpu.VMEM((2, TOK, 4 * HD), BF),
        pltpu.VMEM((2, 1, TOK), I32),
        pltpu.VMEM((3, TOK, LOCAL * HD), BF),
        pltpu.VMEM((1024, 2 * TOK), BF),
        pltpu.VMEM((8, 8, 16, 3 * HD), BF),
        pltpu.VMEM((8, 8, 16, 3 * HD), BF),
        pltpu.VMEM((8, 8, 16, 3 * HD), BF),
        pltpu.VMEM((8, 8, 16, HD), BF),
        pltpu.VMEM((8, 8, 16, HD), BF),
        pltpu.VMEM((8, 8, 16, HD), BF),
        pltpu.VMEM((2, TOK, HD), BF),
        pltpu.VMEM((GROUPS, TOK, LOCAL * HD), BF),
        pltpu.VMEM((GROUPS, 2, TOK, HD), BF),
        pltpu.VMEM((2, TOK, LOCAL * HD), BF),
        pltpu.VMEM((2, 8, 4, 16, 32 * HD), BF),
        pltpu.VMEM((TOK, 1024), F32),
    ]
    scratch += [pltpu.SemaphoreType.DMA(shape) if shape else pltpu.SemaphoreType.DMA for shape in sems]
    return pl.pallas_call(
        kernel,
        out_shape=jax.ShapeDtypeStruct((TOK, 1024), BF),
        in_specs=[pl.BlockSpec(memory_space=pltpu.HBM)] * 5,
        out_specs=pl.BlockSpec(memory_space=pltpu.VMEM),
        scratch_shapes=scratch,
        compiler_params=pltpu.CompilerParams(
            collective_id=0, has_side_effects=True, vmem_limit_bytes=60 * 2**20
        ),
        cost_estimate=pl.CostEstimate(flops=4 * 10**9, bytes_accessed=3 * 2**20, transcendentals=2 * 10**6),
    )(routed_qkv, local_qkv, cluster_ids.transpose(0, 2, 1), wo_routed.T, wo_local.T)


def solution(mesh):
    placed = (
        P(None, "seq", "head"),
        P(None, "seq", "head"),
        P("head", "seq", None),
        P("head", "seq"),
        P("head", "seq"),
    )
    return jax.shard_map(
        on_device, mesh=mesh, in_specs=placed, out_specs=P("seq", "head"), check_vma=False
    )
```

```python
import functools
import math

import jax
import jax.numpy as jnp
from jax import lax
from jax.experimental import pallas as pl
from jax.experimental.pallas import tpu as pltpu
from jax.sharding import PartitionSpec as P

HD = 128
TOK = 256
LOCAL = 6
SIDE = 8
GROUPS = 4
EMPTY = 128.0
NEVER = -1e30
SCALE = 1.0 / math.sqrt(HD)
BF = jnp.bfloat16
F32 = jnp.float32
I32 = jnp.int32
NT = (((1,), (1,)), ((), ()))
NN = (((1,), (0,)), ((), ()))
TN = (((0,), (0,)), ((), ()))


def dot(a, b, dims):
    return lax.dot_general(a, b, dims, preferred_element_type=F32)


def iota(shape, axis):
    return lax.broadcasted_iota(I32, shape, axis)


def each(low, high, body):
    for j in range(low, high):
        body(j)


def div(a, b):
    if isinstance(a, int):
        return a // b
    return lax.div(a, jnp.int32(b))


def rem(a, b):
    if isinstance(a, int):
        return a % b
    return lax.rem(a, jnp.int32(b))


def kernel(
    routed, local_in, ids, wr, wl, out,
    own_x, own_ids, local, place, sent, via, got, answer, back, final, picked, acts, routed_acts, halo,
    wt, summed,
    in_s, a0_s, a0_r, halo_s, halo_r, wx_s, wx_r, p1_s, p1_r, p2_s, p2_r, w1_s, w1_r,
    ring_s, ring_r, sib_s, sib_r, q1_s, q1_r, q2_s, q2_r, xl_s, xl_r, xr_s, xr_r,
):
    h = lax.axis_index("head")
    s = lax.axis_index("seq")
    c = rem(s, 2)
    oc = 1 - c
    chip = div(s, 2)
    z = rem(chip, SIDE)
    y = div(chip, SIDE)
    u = z * oc + y * c
    w = y * oc + z * c
    sibling = s + 1 - 2 * c

    def seq_yz(yy, zz):
        return (yy * SIDE + zz) * 2 + c

    def seq_uw(uu, ww):
        return seq_yz(ww * oc + uu * c, uu * oc + ww * c)

    def to_seq(src, dst, ss, rs, seq):
        return pltpu.make_async_remote_copy(
            src_ref=src, dst_ref=dst, send_sem=ss, recv_sem=rs,
            device_id={"seq": seq}, device_id_type=pl.DeviceIdType.MESH,
        )

    def to_any(src, dst, ss, rs, seq, head):
        return pltpu.make_async_remote_copy(
            src_ref=src, dst_ref=dst, send_sem=ss, recv_sem=rs,
            device_id={"seq": seq, "head": head}, device_id_type=pl.DeviceIdType.MESH,
        )

    def hello(seq, head):
        pl.semaphore_signal(
            barrier, inc=1, device_id={"seq": seq, "head": head}, device_id_type=pl.DeviceIdType.MESH
        )

    def w_target(r):
        return div(y, 2), rem(y, 2) * 4 + c * 2 + r, div(h, 2)

    def w_source(i):
        return 2 * c + i, 2 * h + div(y, 4), div(rem(y, 4), 2)

    def target_is_me(r):
        head, row, core = w_target(r)
        return (head == h) & (row == y) & (core == c)

    def source_is_me(i):
        head, row, core = w_source(i)
        return (head == h) & (row == y) & (core == c)

    barrier = pltpu.get_barrier_semaphore()

    def greet(j):
        for target in (seq_uw(rem(u + j, SIDE), w), seq_uw(u, rem(w + j, SIDE))):
            pl.semaphore_signal(barrier, inc=1, device_id={"seq": target}, device_id_type=pl.DeviceIdType.MESH)

    each(1, SIDE, greet)
    pl.semaphore_signal(barrier, inc=1, device_id={"seq": sibling}, device_id_type=pl.DeviceIdType.MESH)
    for j in range(1, GROUPS):
        hello(s, rem(h + j, GROUPS))
        hello(sibling, rem(h + j, GROUPS))
    for i in range(2):
        head, row, core = w_source(i)

        @pl.when(jnp.logical_not(source_is_me(i)))
        def _():
            hello((row * SIDE + z) * 2 + core, head)

    @pl.when((c == 0) & (s > 0))
    def _():
        pl.semaphore_signal(barrier, inc=1, device_id={"seq": s - 1}, device_id_type=pl.DeviceIdType.MESH)

    selves = jnp.where(target_is_me(0) | target_is_me(1), 1, 0)
    expected = 2 * (SIDE - 1) + 1 + 2 * (GROUPS - 1) + 2
    pl.semaphore_wait(barrier, expected + c * (1 - div(s, 2 * SIDE * SIDE - 1)) - selves)

    def lanes(first, count):
        return pl.ds(pl.multiple_of(first, HD), count)

    halo_copy = to_seq(local_in.at[pl.ds(1, 2)], halo, halo_s, halo_r, s + 1)

    pieces = ((wr, 0, 2 * HD), (wl, 4 * HD, LOCAL * HD))

    def w_landing(row, head, piece):
        _, first, count = pieces[piece]
        at = lanes(div(head, 2) * 16 * HD + first + rem(head, 2) * count, count)
        return wt.at[div(row, 4), z, rem(row, 4), :, at]

    def w_send(r, piece):
        head, row, core = w_target(r)
        src = pieces[piece][0].at[pl.ds(r * 16, 16)]
        return to_any(
            src, w_landing(row, h, piece), wx_s.at[r, piece], wx_r.at[rem(h, 2), piece],
            (row * SIDE + z) * 2 + core, head,
        )

    def w_keep(r, piece):
        src = pieces[piece][0].at[pl.ds(r * 16, 16)]
        return pltpu.make_async_copy(src, w_landing(w_target(r)[1], h, piece), in_s.at[piece])

    def w_take(i, piece):
        head, row, core = w_source(i)
        src = pieces[piece][0].at[pl.ds(0, 16)]
        return to_any(
            src, w_landing(y, head, piece), wx_s.at[0, piece], wx_r.at[i, piece],
            (row * SIDE + z) * 2 + core, head,
        )

    for r in range(2):
        me = target_is_me(r)

        @pl.when(me)
        def _():
            for piece in range(2):
                w_keep(r, piece).start()

        @pl.when(jnp.logical_not(me))
        def _():
            for piece in range(2):
                w_send(r, piece).start()

    def head_rows(j, core):
        return routed.at[j, :, pl.ds(pl.multiple_of(core * HD, HD), HD)]

    def a0(core):
        copies = [
            to_seq(head_rows(j, oc), own_x.at[core, :, pl.ds(j * HD, HD)], a0_s.at[j], a0_r.at[j], sibling)
            for j in range(3)
        ]
        return copies + [to_seq(ids.at[oc], own_ids.at[core], a0_s.at[3], a0_r.at[3], sibling)]

    for copy in a0(c):
        copy.start()
    own = [
        pltpu.make_async_copy(head_rows(j, c), own_x.at[c, :, pl.ds(j * HD, HD)], in_s.at[2 + j])
        for j in range(3)
    ]
    own.append(pltpu.make_async_copy(ids.at[c], own_ids.at[c], in_s.at[5]))
    own.append(pltpu.make_async_copy(local_in, local, in_s.at[6]))
    for copy in own:
        copy.start()
    own_x[:, :, 3 * HD :] = jnp.ones((2, TOK, HD), BF)

    def block_of(core, yy, zz):
        return wt.at[div(yy, 4), zz, rem(yy, 4), :, pl.ds(core * 16 * HD, 16 * HD)]

    def w1(j, core, sending):
        if core == 0:
            target = seq_yz(y, rem(z + j, SIDE))
            here = rem(z + SIDE - j, SIDE)
            blk = block_of(core, y, z) if sending else block_of(core, y, here)
        else:
            target = seq_yz(rem(y + j, SIDE), z)
            here = rem(y + SIDE - j, SIDE)
            blk = block_of(core, y, z) if sending else block_of(core, here, z)
        return to_seq(blk, blk, w1_s.at[j], w1_r.at[j], target)

    def by_core(body):
        for core in range(2):
            pl.when(c == core)(functools.partial(body, core))

    for copy in own[:4]:
        copy.wait()
    for copy in a0(oc):
        copy.wait_recv()

    def rows_of(b):
        cluster = own_ids[b]
        name = cluster.astype(F32)
        first_row = jnp.where(iota((8, TOK), 0) == 0, jnp.broadcast_to(name, (8, TOK)), 0.0).astype(BF)
        down = dot(first_row, jnp.ones((8, TOK), BF), TN)
        earlier = (down == name) & (iota((TOK, TOK), 0) < iota((TOK, TOK), 1))
        rank = jnp.sum(jnp.where(earlier, 1.0, 0.0), axis=0, keepdims=True).astype(I32)
        owner = cluster >> 2
        turned = (owner & 7) * SIDE + (owner >> 3)
        goes = turned * oc + owner * c
        return goes * 16 + b * 8 + (cluster & 3) * 2 + rank

    slot = jnp.concatenate([rows_of(0), rows_of(1)], axis=1)
    both = own_x[...].reshape(2 * TOK, 4 * HD)

    def fill(i):
        hot = (iota((256, 2 * TOK), 0) + i * 256 == slot).astype(F32).astype(BF)
        place[pl.ds(i * 256, 256)] = hot
        rows = dot(hot, both, NN)
        lead = (1.0 - rows[:, 3 * HD :]) * EMPTY
        rows = jnp.concatenate([rows[:, :HD], rows[:, HD : 2 * HD] + lead, rows[:, 2 * HD : 3 * HD]], axis=1)
        sent[pl.ds(2 * i, 2)] = rows.astype(BF).reshape(2, SIDE, 16, 3 * HD)

    each(0, 4, fill)

    def p1(j, sending):
        there, here = rem(u + j, SIDE), rem(u + SIDE - j, SIDE)
        dst = via.at[u] if sending else via.at[here]
        return to_seq(sent.at[there], dst, p1_s.at[j], p1_r.at[j], seq_uw(there, w))

    each(1, SIDE, lambda j: p1(j, True).start())
    via[u] = sent[u]

    for i in range(2):
        me = source_is_me(i)
        for piece in range(2):

            @pl.when(me)
            def _():
                r = rem(y, 2)
                for value in range(2):

                    @pl.when(r == value)
                    def _():
                        w_keep(value, piece).wait()

            @pl.when(jnp.logical_not(me))
            def _():
                w_take(i, piece).wait_recv()

    def w1_start(core):
        each(1, SIDE, lambda j: w1(j, core, True).start())

    by_core(w1_start)

    @pl.when(s < 2 * SIDE * SIDE - 1)
    def _():
        halo_copy.start()


    def w1_take(core):
        each(1, SIDE, lambda j: w1(j, core, False).wait_recv())

    by_core(w1_take)

    def blocks(core, place_on, first=0, count=16 * HD):
        at = rem(place_on + SIDE, SIDE)
        part = pl.ds(core * 16 * HD + first, count)
        if core == 0:
            return wt.at[div(at, 4), :, rem(at, 4), :, part]
        return wt.at[:, at, :, :, part]

    def ring(k, way, part, core, sending):
        coord = y if core == 0 else z
        sign = 1 - 2 * way
        at = coord - sign * (k - 1) if sending else coord - sign * k
        blk = blocks(core, at, part * 8 * HD, 8 * HD)
        to = rem(coord + sign + SIDE, SIDE)
        target = seq_yz(to, z) if core == 0 else seq_yz(y, to)
        return to_seq(blk, blk, ring_s.at[k, way, part], ring_r.at[k, way, part], target)

    def goes(k, part, core):
        if k < SIDE // 2:
            return (0, 1)
        return (part,) if core == 0 else (1,)

    def sib(k, way, path):
        coord = y if path == 0 else z
        blk = blocks(path, coord - (1 - 2 * way) * k)
        return to_seq(blk, blk, sib_s.at[k, way], sib_r.at[k, way], sibling)

    def ways(k):
        return (0,) if k in (0, SIDE // 2) else (0, 1)

    def ring_step(k, part):
        def body(core):
            if k > 1:
                for way in goes(k - 1, part, core):
                    ring(k - 1, way, part, core, False).wait_recv()
            if k <= SIDE // 2:
                for way in goes(k, part, core):
                    ring(k, way, part, core, True).start()
            if part == 1:
                for way in ways(k - 1):
                    sib(k - 1, way, core).start()

        by_core(body)

    def sib_wait(k):
        def body(core):
            for way in ways(k):
                sib(k, way, 1 - core).wait_recv()

        by_core(body)

    ring_step(1, 0)
    ring_step(1, 1)

    each(1, SIDE, lambda j: p1(j, False).wait_recv())

    def p2(j, sending, core):
        there, here = rem(w + j, SIDE), rem(w + SIDE - j, SIDE)
        at = w if sending else here
        dst = got.at[at] if core == 0 else got.at[:, at]
        return to_seq(via.at[:, there], dst, p2_s.at[j], p2_r.at[j], seq_uw(u, there))

    def p2_start(core):
        each(1, SIDE, lambda j: p2(j, True, core).start())

        def keep(i):
            if core == 0:
                got[w, i] = via[i, w]
            else:
                got[i, w] = via[i, w]

        each(0, SIDE, keep)

    by_core(p2_start)
    ring_step(2, 0)
    ring_step(2, 1)

    own[4].wait()

    @pl.when(s > 0)
    def _():
        halo_copy.wait_recv()

    @pl.when(s == 0)
    def _():
        halo[...] = jnp.zeros_like(halo)

    own_side = iota((TOK, TOK), 1) <= iota((TOK, TOK), 0)
    shift = jnp.where(s > 0, jnp.float32(0.0), jnp.float32(NEVER))

    def window(n):
        cols = pl.ds(n * HD, HD)
        query = local[0, :, cols]
        here = dot(query, local[1, :, cols], NT) * SCALE
        before = dot(query, halo[0, :, cols], NT) * SCALE + shift
        scores = jnp.where(own_side, here, before)
        raised = jnp.exp(scores - jnp.max(scores, axis=1, keepdims=True))
        weights = raised * (1.0 / jnp.sum(raised, axis=1, keepdims=True))
        near = jnp.where(own_side, weights, 0.0).astype(BF)
        far = jnp.where(own_side, 0.0, weights).astype(BF)
        result = dot(near, local[2, :, cols], NN) + dot(far, halo[1, :, cols], NN)
        acts[h, :, pl.ds(n * HD, HD)] = result.astype(BF)

    each(0, LOCAL, window)

    def xl(j, sending):
        there, here = rem(h + j, GROUPS), rem(h + GROUPS - j, GROUPS)
        dst = acts.at[h] if sending else acts.at[here]
        return to_any(acts.at[h], dst, xl_s.at[j], xl_r.at[j], s, there)

    each(1, GROUPS, lambda j: xl(j, True).start())


    def p2_take(core):
        each(1, SIDE, lambda j: p2(j, False, core).wait_recv())

    by_core(p2_take)

    def code_of(r):
        return ((r >> 1) & 3) * 4096 + (r >> 4) * 4 + ((r >> 3) & 1) * 2 + (r & 1)

    keys = got[:, :, :, HD : 2 * HD].reshape(1024, HD)
    lane_zero = (iota((8, HD), 1) == 0).astype(F32).astype(BF)
    lead_key = dot(lane_zero, keys, NT)[0:1]
    key_code = jnp.where(lead_key < 0.75 * EMPTY, code_of(iota((8, 1024), 1))[0:1], 1 << 20)

    def cluster_rows(last, i):
        keys = got[: last // 128, :, :, HD : 2 * HD].reshape(last, HD)
        values = got[: last // 128, :, :, 2 * HD :].reshape(last, HD)
        query = got[pl.ds(2 * i, 2), :, :, 0:HD].reshape(256, HD)
        scores = dot(query, keys, NT) * SCALE
        ahead = code_of(iota((256, HD), 0) + i * 256)[:, 0:1] - key_code[:, :last]
        scores = jnp.where((ahead >= 0) & (ahead < 256), scores, NEVER)
        raised = jnp.exp(scores - jnp.max(scores, axis=1, keepdims=True))
        weights = (raised * (1.0 / jnp.sum(raised, axis=1, keepdims=True))).astype(BF)
        answer[pl.ds(2 * i, 2)] = dot(weights, values, NN).astype(BF).reshape(2, SIDE, 16, HD)

    for i in range(4):
        cluster_rows((i + 1) * 256, i)

    def q1(j, sending, core):
        there, here = rem(w + j, SIDE), rem(w + SIDE - j, SIDE)
        src = answer.at[there] if core == 0 else answer.at[:, there]
        dst = back.at[w] if sending else back.at[here]
        return to_seq(src, dst, q1_s.at[j], q1_r.at[j], seq_uw(u, there))

    def q1_start(core):
        each(1, SIDE, lambda j: q1(j, True, core).start())

        def keep(i):
            back[w, i] = answer[w, i] if core == 0 else answer[i, w]

        each(0, SIDE, keep)

    by_core(q1_start)


    ring_step(3, 0)
    ring_step(3, 1)

    each(1, SIDE, lambda j: q1(j, False, 0).wait_recv())

    def q2(j, sending):
        there, here = rem(u + j, SIDE), rem(u + SIDE - j, SIDE)
        dst = final.at[u] if sending else final.at[here]
        return to_seq(back.at[:, there], dst, q2_s.at[j], q2_r.at[j], seq_uw(there, w))

    each(1, SIDE, lambda j: q2(j, True).start())

    def keep_final(i):
        final[u, i] = back[i, u]

    each(0, SIDE, keep_final)

    ring_step(4, 0)
    ring_step(4, 1)

    def project(e, zh):
        for part in range(2):
            first = (part * 16 + 4) * HD
            wide = jnp.concatenate([acts[2 * part], acts[2 * part + 1]], axis=1)
            at = pl.ds(first, 2 * LOCAL * HD)
            if part == 0:
                rows = wt[e, :, :, :, at]
            else:
                rows = wt[:, pl.ds(zh * 4, 4), :, :, at]
            share = dot(wide, rows.reshape(512, 2 * LOCAL * HD), NT)
            for n in range(2):
                piece = share[:, n * 256 : (n + 1) * 256]
                if part == 0:
                    summed[0, e, n] = piece
                else:
                    summed[1, n, zh] = piece

    each(1, SIDE, lambda j: q2(j, False).wait_recv())
    tokens = dot(place[...], final[...].reshape(1024, HD), TN).astype(BF)
    picked[0] = tokens[:TOK]
    picked[1] = tokens[TOK:]

    def xr(j, b, sending):
        there, here = rem(h + j, GROUPS), rem(h + GROUPS - j, GROUPS)
        own_side = c * (1 - b) + oc * b
        to = s * (1 - b) + sibling * b
        if sending:
            src, dst = picked.at[own_side], routed_acts.at[h, c]
        else:
            src, dst = picked.at[0], routed_acts.at[here, own_side]
        return to_any(src, dst, xr_s.at[j, b], xr_r.at[j, b], to, there if sending else here)

    for j in range(GROUPS):
        for b in range(2):
            if j or b:
                xr(j, b, True).start()
    routed_acts[h, c] = picked[c]

    for k in range(SIDE // 2):
        sib_wait(k)
    each(1, GROUPS, lambda j: xl(j, False).wait_recv())
    project(div(y, 4), div(z, 4))

    ring_step(5, 0)
    ring_step(5, 1)
    sib_wait(4)
    project(1 - div(y, 4), 1 - div(z, 4))
    for j in range(GROUPS):
        for b in range(2):
            if j or b:
                xr(j, b, False).wait_recv()
    wide = [
        jnp.concatenate([routed_acts[2 * part + g, n] for g in range(2) for n in range(2)], axis=1)
        for part in range(2)
    ]
    for e in range(2):
        for zh in range(2):
            total = summed[0, e, zh] + summed[1, e, zh]
            for part in range(2):
                first = part * 16 * HD
                rows = wt[e, 4 * zh : 4 * zh + 4, :, :, first : first + 4 * HD].reshape(256, 4 * HD)
                total = total + dot(wide[part], rows, NT)
            first = e * 512 + zh * 256
            out[:, first : first + 256] = total.astype(BF)

    for copy in a0(c):
        copy.wait_send()

    @pl.when(s < 2 * SIDE * SIDE - 1)
    def _():
        halo_copy.wait_send()

    for r in range(2):

        @pl.when(jnp.logical_not(target_is_me(r)))
        def _():
            for piece in range(2):
                w_send(r, piece).wait_send()

    def left(j):
        p1(j, True).wait_send()
        q2(j, True).wait_send()

    each(1, SIDE, left)

    def drain(core):
        def left(j):
            p2(j, True, core).wait_send()
            q1(j, True, core).wait_send()

        each(1, SIDE, left)

        each(1, SIDE, lambda j: w1(j, core, True).wait_send())

        for k in range(1, SIDE // 2 + 1):
            for part in range(2):
                for way in goes(k, part, core):
                    ring(k, way, part, core, True).wait_send()
        for k in range(SIDE // 2 + 1):
            for way in ways(k):
                sib(k, way, core).wait_send()

    by_core(drain)
    each(1, GROUPS, lambda j: xl(j, True).wait_send())
    for j in range(GROUPS):
        for b in range(2):
            if j or b:
                xr(j, b, True).wait_send()


def on_device(routed_qkv, local_qkv, cluster_ids, wo_routed, wo_local):
    sems = [
        (7,), (4,), (4,), (), (), (2, 2), (2, 2), (8,), (8,), (8,), (8,), (8,), (8,),
        (5, 2, 2), (5, 2, 2), (5, 2), (5, 2), (8,), (8,), (8,), (8,),
        (4,), (4,), (4, 2), (4, 2),
    ]
    scratch = [
        pltpu.VMEM((2, TOK, 4 * HD), BF),
        pltpu.VMEM((2, 1, TOK), I32),
        pltpu.VMEM((3, TOK, LOCAL * HD), BF),
        pltpu.VMEM((1024, 2 * TOK), BF),
        pltpu.VMEM((8, 8, 16, 3 * HD), BF),
        pltpu.VMEM((8, 8, 16, 3 * HD), BF),
        pltpu.VMEM((8, 8, 16, 3 * HD), BF),
        pltpu.VMEM((8, 8, 16, HD), BF),
        pltpu.VMEM((8, 8, 16, HD), BF),
        pltpu.VMEM((8, 8, 16, HD), BF),
        pltpu.VMEM((2, TOK, HD), BF),
        pltpu.VMEM((GROUPS, TOK, LOCAL * HD), BF),
        pltpu.VMEM((GROUPS, 2, TOK, HD), BF),
        pltpu.VMEM((2, TOK, LOCAL * HD), BF),
        pltpu.VMEM((2, 8, 4, 16, 32 * HD), BF),
        pltpu.VMEM((2, 2, 2, TOK, 256), F32),
    ]
    scratch += [pltpu.SemaphoreType.DMA(shape) if shape else pltpu.SemaphoreType.DMA for shape in sems]
    return pl.pallas_call(
        kernel,
        out_shape=jax.ShapeDtypeStruct((TOK, 1024), BF),
        in_specs=[pl.BlockSpec(memory_space=pltpu.HBM)] * 5,
        out_specs=pl.BlockSpec(memory_space=pltpu.VMEM),
        scratch_shapes=scratch,
        compiler_params=pltpu.CompilerParams(
            collective_id=0, has_side_effects=True, vmem_limit_bytes=60 * 2**20
        ),
        cost_estimate=pl.CostEstimate(flops=4 * 10**9, bytes_accessed=3 * 2**20, transcendentals=2 * 10**6),
    )(routed_qkv, local_qkv, cluster_ids.transpose(0, 2, 1), wo_routed.T, wo_local.T)


def solution(mesh):
    placed = (
        P(None, "seq", "head"),
        P(None, "seq", "head"),
        P("head", "seq", None),
        P("head", "seq"),
        P("head", "seq"),
    )
    return jax.shard_map(
        on_device, mesh=mesh, in_specs=placed, out_specs=P("seq", "head"), check_vma=False
    )
```

```python
import functools
import math

import jax
import jax.numpy as jnp
from jax import lax
from jax.experimental import pallas as pl
from jax.experimental.pallas import tpu as pltpu
from jax.sharding import PartitionSpec as P

HD = 128
TOK = 256
LOCAL = 6
SIDE = 8
GROUPS = 4
BOTH_WAYS = (4, 3, 5, 2, 6, 1, 7)
EMPTY = 128.0
NEVER = -1e30
SCALE = 1.0 / math.sqrt(HD)
BF = jnp.bfloat16
F32 = jnp.float32
I32 = jnp.int32
NT = (((1,), (1,)), ((), ()))
NN = (((1,), (0,)), ((), ()))
TN = (((0,), (0,)), ((), ()))


def dot(a, b, dims):
    return lax.dot_general(a, b, dims, preferred_element_type=F32)


def iota(shape, axis):
    return lax.broadcasted_iota(I32, shape, axis)


def each(low, high, body):
    for j in BOTH_WAYS if (low, high) == (1, SIDE) else range(low, high):
        body(j)


def div(a, b):
    if isinstance(a, int):
        return a // b
    return lax.div(a, jnp.int32(b))


def rem(a, b):
    if isinstance(a, int):
        return a % b
    return lax.rem(a, jnp.int32(b))


def kernel(
    routed, local_in, ids, wr, wl, out,
    own_x, own_ids, local, place, sent, via, got, answer, back, final, picked, acts, routed_acts, halo,
    wt, summed,
    in_s, a0_s, a0_r, halo_s, halo_r, wx_s, wx_r, p1_s, p1_r, p2_s, p2_r, w1_s, w1_r,
    ring_s, ring_r, sib_s, sib_r, q1_s, q1_r, q2_s, q2_r, xl_s, xl_r, xr_s, xr_r,
):
    h = lax.axis_index("head")
    s = lax.axis_index("seq")
    c = rem(s, 2)
    oc = 1 - c
    chip = div(s, 2)
    z = rem(chip, SIDE)
    y = div(chip, SIDE)
    u = z * oc + y * c
    w = y * oc + z * c
    sibling = s + 1 - 2 * c

    def seq_yz(yy, zz):
        return (yy * SIDE + zz) * 2 + c

    def seq_uw(uu, ww):
        return seq_yz(ww * oc + uu * c, uu * oc + ww * c)

    def to_seq(src, dst, ss, rs, seq):
        return pltpu.make_async_remote_copy(
            src_ref=src, dst_ref=dst, send_sem=ss, recv_sem=rs,
            device_id={"seq": seq}, device_id_type=pl.DeviceIdType.MESH,
        )

    def to_any(src, dst, ss, rs, seq, head):
        return pltpu.make_async_remote_copy(
            src_ref=src, dst_ref=dst, send_sem=ss, recv_sem=rs,
            device_id={"seq": seq, "head": head}, device_id_type=pl.DeviceIdType.MESH,
        )

    def hello(seq, head):
        pl.semaphore_signal(
            barrier, inc=1, device_id={"seq": seq, "head": head}, device_id_type=pl.DeviceIdType.MESH
        )

    def w_target(r):
        return div(y, 2), rem(y, 2) * 4 + c * 2 + r, div(h, 2)

    def w_source(i):
        return 2 * c + i, 2 * h + div(y, 4), div(rem(y, 4), 2)

    def target_is_me(r):
        head, row, core = w_target(r)
        return (head == h) & (row == y) & (core == c)

    def source_is_me(i):
        head, row, core = w_source(i)
        return (head == h) & (row == y) & (core == c)

    barrier = pltpu.get_barrier_semaphore()

    def greet(j):
        for target in (seq_uw(rem(u + j, SIDE), w), seq_uw(u, rem(w + j, SIDE))):
            pl.semaphore_signal(barrier, inc=1, device_id={"seq": target}, device_id_type=pl.DeviceIdType.MESH)

    each(1, SIDE, greet)
    pl.semaphore_signal(barrier, inc=1, device_id={"seq": sibling}, device_id_type=pl.DeviceIdType.MESH)
    for j in range(1, GROUPS):
        hello(s, rem(h + j, GROUPS))
        hello(sibling, rem(h + j, GROUPS))
    for i in range(2):
        head, row, core = w_source(i)

        @pl.when(jnp.logical_not(source_is_me(i)))
        def _():
            hello((row * SIDE + z) * 2 + core, head)

    @pl.when((c == 0) & (s > 0))
    def _():
        pl.semaphore_signal(barrier, inc=1, device_id={"seq": s - 1}, device_id_type=pl.DeviceIdType.MESH)

    selves = jnp.where(target_is_me(0) | target_is_me(1), 1, 0)
    expected = 2 * (SIDE - 1) + 1 + 2 * (GROUPS - 1) + 2
    pl.semaphore_wait(barrier, expected + c * (1 - div(s, 2 * SIDE * SIDE - 1)) - selves)

    def lanes(first, count):
        return pl.ds(pl.multiple_of(first, HD), count)

    halo_copy = to_seq(local_in.at[pl.ds(1, 2)], halo, halo_s, halo_r, s + 1)

    pieces = ((wr, 0, 2 * HD), (wl, 4 * HD, LOCAL * HD))

    def w_landing(row, head, piece):
        _, first, count = pieces[piece]
        at = lanes(div(head, 2) * 16 * HD + first + rem(head, 2) * count, count)
        return wt.at[div(row, 4), z, rem(row, 4), :, at]

    def w_send(r, piece):
        head, row, core = w_target(r)
        src = pieces[piece][0].at[pl.ds(r * 16, 16)]
        return to_any(
            src, w_landing(row, h, piece), wx_s.at[r, piece], wx_r.at[rem(h, 2), piece],
            (row * SIDE + z) * 2 + core, head,
        )

    def w_keep(r, piece):
        src = pieces[piece][0].at[pl.ds(r * 16, 16)]
        return pltpu.make_async_copy(src, w_landing(w_target(r)[1], h, piece), in_s.at[piece])

    def w_take(i, piece):
        head, row, core = w_source(i)
        src = pieces[piece][0].at[pl.ds(0, 16)]
        return to_any(
            src, w_landing(y, head, piece), wx_s.at[0, piece], wx_r.at[i, piece],
            (row * SIDE + z) * 2 + core, head,
        )

    for r in range(2):
        me = target_is_me(r)

        @pl.when(me)
        def _():
            for piece in range(2):
                w_keep(r, piece).start()

        @pl.when(jnp.logical_not(me))
        def _():
            for piece in range(2):
                w_send(r, piece).start()

    def head_rows(j, core):
        return routed.at[j, :, pl.ds(pl.multiple_of(core * HD, HD), HD)]

    def a0(core):
        copies = [
            to_seq(head_rows(j, oc), own_x.at[core, :, pl.ds(j * HD, HD)], a0_s.at[j], a0_r.at[j], sibling)
            for j in range(3)
        ]
        return copies + [to_seq(ids.at[oc], own_ids.at[core], a0_s.at[3], a0_r.at[3], sibling)]

    for copy in a0(c):
        copy.start()
    own = [
        pltpu.make_async_copy(head_rows(j, c), own_x.at[c, :, pl.ds(j * HD, HD)], in_s.at[2 + j])
        for j in range(3)
    ]
    own.append(pltpu.make_async_copy(ids.at[c], own_ids.at[c], in_s.at[5]))
    own.append(pltpu.make_async_copy(local_in, local, in_s.at[6]))
    for copy in own:
        copy.start()
    own_x[:, :, 3 * HD :] = jnp.ones((2, TOK, HD), BF)

    def block_of(core, yy, zz):
        return wt.at[div(yy, 4), zz, rem(yy, 4), :, pl.ds(core * 16 * HD, 16 * HD)]

    def w1(j, core, sending):
        if core == 0:
            target = seq_yz(y, rem(z + j, SIDE))
            here = rem(z + SIDE - j, SIDE)
            blk = block_of(core, y, z) if sending else block_of(core, y, here)
        else:
            target = seq_yz(rem(y + j, SIDE), z)
            here = rem(y + SIDE - j, SIDE)
            blk = block_of(core, y, z) if sending else block_of(core, here, z)
        return to_seq(blk, blk, w1_s.at[j], w1_r.at[j], target)

    def by_core(body):
        for core in range(2):
            pl.when(c == core)(functools.partial(body, core))

    for copy in own[:4]:
        copy.wait()
    for copy in a0(oc):
        copy.wait_recv()

    def rows_of(b):
        cluster = own_ids[b]
        name = cluster.astype(F32)
        first_row = jnp.where(iota((8, TOK), 0) == 0, jnp.broadcast_to(name, (8, TOK)), 0.0).astype(BF)
        down = dot(first_row, jnp.ones((8, TOK), BF), TN)
        earlier = (down == name) & (iota((TOK, TOK), 0) < iota((TOK, TOK), 1))
        rank = jnp.sum(jnp.where(earlier, 1.0, 0.0), axis=0, keepdims=True).astype(I32)
        owner = cluster >> 2
        turned = (owner & 7) * SIDE + (owner >> 3)
        goes = turned * oc + owner * c
        return goes * 16 + b * 8 + (cluster & 3) * 2 + rank

    slot = jnp.concatenate([rows_of(0), rows_of(1)], axis=1)
    both = own_x[...].reshape(2 * TOK, 4 * HD)

    def fill(i):
        hot = (iota((256, 2 * TOK), 0) + i * 256 == slot).astype(F32).astype(BF)
        place[pl.ds(i * 256, 256)] = hot
        rows = dot(hot, both, NN)
        lead = (1.0 - rows[:, 3 * HD :]) * EMPTY
        rows = jnp.concatenate([rows[:, :HD], rows[:, HD : 2 * HD] + lead, rows[:, 2 * HD : 3 * HD]], axis=1)
        sent[pl.ds(2 * i, 2)] = rows.astype(BF).reshape(2, SIDE, 16, 3 * HD)

    each(0, 4, fill)

    def p1(j, sending):
        there, here = rem(u + j, SIDE), rem(u + SIDE - j, SIDE)
        dst = via.at[u] if sending else via.at[here]
        return to_seq(sent.at[there], dst, p1_s.at[j], p1_r.at[j], seq_uw(there, w))

    each(1, SIDE, lambda j: p1(j, True).start())
    via[u] = sent[u]

    for i in range(2):
        me = source_is_me(i)
        for piece in range(2):

            @pl.when(me)
            def _():
                r = rem(y, 2)
                for value in range(2):

                    @pl.when(r == value)
                    def _():
                        w_keep(value, piece).wait()

            @pl.when(jnp.logical_not(me))
            def _():
                w_take(i, piece).wait_recv()

    def w1_start(core):
        each(1, SIDE, lambda j: w1(j, core, True).start())

    by_core(w1_start)

    @pl.when(s < 2 * SIDE * SIDE - 1)
    def _():
        halo_copy.start()


    def w1_take(core):
        each(1, SIDE, lambda j: w1(j, core, False).wait_recv())

    by_core(w1_take)

    def blocks(core, place_on, first=0, count=16 * HD):
        at = rem(place_on + SIDE, SIDE)
        part = pl.ds(core * 16 * HD + first, count)
        if core == 0:
            return wt.at[div(at, 4), :, rem(at, 4), :, part]
        return wt.at[:, at, :, :, part]

    def ring(k, way, part, core, sending):
        coord = y if core == 0 else z
        sign = 1 - 2 * way
        at = coord - sign * (k - 1) if sending else coord - sign * k
        blk = blocks(core, at, part * 8 * HD, 8 * HD)
        to = rem(coord + sign + SIDE, SIDE)
        target = seq_yz(to, z) if core == 0 else seq_yz(y, to)
        return to_seq(blk, blk, ring_s.at[k, way, part], ring_r.at[k, way, part], target)

    def goes(k, part, core):
        if k < SIDE // 2:
            return (0, 1)
        return (part,) if core == 0 else (1,)

    def sib(k, way, path):
        coord = y if path == 0 else z
        blk = blocks(path, coord - (1 - 2 * way) * k)
        return to_seq(blk, blk, sib_s.at[k, way], sib_r.at[k, way], sibling)

    def ways(k):
        return (0,) if k in (0, SIDE // 2) else (0, 1)

    def ring_step(k, part):
        def body(core):
            if k > 1:
                for way in goes(k - 1, part, core):
                    ring(k - 1, way, part, core, False).wait_recv()
            if k <= SIDE // 2:
                for way in goes(k, part, core):
                    ring(k, way, part, core, True).start()
            if part == 1:
                for way in ways(k - 1):
                    sib(k - 1, way, core).start()

        by_core(body)

    def sib_wait(k):
        def body(core):
            for way in ways(k):
                sib(k, way, 1 - core).wait_recv()

        by_core(body)

    ring_step(1, 0)
    ring_step(1, 1)

    each(1, SIDE, lambda j: p1(j, False).wait_recv())

    def p2(j, sending, core):
        there, here = rem(w + j, SIDE), rem(w + SIDE - j, SIDE)
        at = w if sending else here
        dst = got.at[at] if core == 0 else got.at[:, at]
        return to_seq(via.at[:, there], dst, p2_s.at[j], p2_r.at[j], seq_uw(u, there))

    def p2_start(core):
        each(1, SIDE, lambda j: p2(j, True, core).start())

        def keep(i):
            if core == 0:
                got[w, i] = via[i, w]
            else:
                got[i, w] = via[i, w]

        each(0, SIDE, keep)

    by_core(p2_start)
    ring_step(2, 0)
    ring_step(2, 1)

    own[4].wait()

    @pl.when(s > 0)
    def _():
        halo_copy.wait_recv()

    @pl.when(s == 0)
    def _():
        halo[...] = jnp.zeros_like(halo)

    own_side = iota((TOK, TOK), 1) <= iota((TOK, TOK), 0)
    shift = jnp.where(s > 0, jnp.float32(0.0), jnp.float32(NEVER))

    def window(n):
        cols = pl.ds(n * HD, HD)
        query = local[0, :, cols]
        here = dot(query, local[1, :, cols], NT) * SCALE
        before = dot(query, halo[0, :, cols], NT) * SCALE + shift
        scores = jnp.where(own_side, here, before)
        raised = jnp.exp(scores - jnp.max(scores, axis=1, keepdims=True))
        weights = raised * (1.0 / jnp.sum(raised, axis=1, keepdims=True))
        near = jnp.where(own_side, weights, 0.0).astype(BF)
        far = jnp.where(own_side, 0.0, weights).astype(BF)
        result = dot(near, local[2, :, cols], NN) + dot(far, halo[1, :, cols], NN)
        acts[h, :, pl.ds(n * HD, HD)] = result.astype(BF)

    each(0, LOCAL, window)

    def xl(j, sending):
        there, here = rem(h + j, GROUPS), rem(h + GROUPS - j, GROUPS)
        dst = acts.at[h] if sending else acts.at[here]
        return to_any(acts.at[h], dst, xl_s.at[j], xl_r.at[j], s, there)

    each(1, GROUPS, lambda j: xl(j, True).start())


    def p2_take(core):
        each(1, SIDE, lambda j: p2(j, False, core).wait_recv())

    by_core(p2_take)

    def code_of(r):
        return ((r >> 1) & 3) * 4096 + (r >> 4) * 4 + ((r >> 3) & 1) * 2 + (r & 1)

    keys = got[:, :, :, HD : 2 * HD].reshape(1024, HD)
    lane_zero = (iota((8, HD), 1) == 0).astype(F32).astype(BF)
    lead_key = dot(lane_zero, keys, NT)[0:1]
    key_code = jnp.where(lead_key < 0.75 * EMPTY, code_of(iota((8, 1024), 1))[0:1], 1 << 20)

    def cluster_rows(last, i):
        keys = got[: last // 128, :, :, HD : 2 * HD].reshape(last, HD)
        values = got[: last // 128, :, :, 2 * HD :].reshape(last, HD)
        query = got[pl.ds(2 * i, 2), :, :, 0:HD].reshape(256, HD)
        scores = dot(query, keys, NT) * SCALE
        ahead = code_of(iota((256, HD), 0) + i * 256)[:, 0:1] - key_code[:, :last]
        scores = jnp.where((ahead >= 0) & (ahead < 256), scores, NEVER)
        raised = jnp.exp(scores - jnp.max(scores, axis=1, keepdims=True))
        weights = (raised * (1.0 / jnp.sum(raised, axis=1, keepdims=True))).astype(BF)
        answer[pl.ds(2 * i, 2)] = dot(weights, values, NN).astype(BF).reshape(2, SIDE, 16, HD)

    for i in range(4):
        cluster_rows((i + 1) * 256, i)

    def q1(j, sending, core):
        there, here = rem(w + j, SIDE), rem(w + SIDE - j, SIDE)
        src = answer.at[there] if core == 0 else answer.at[:, there]
        dst = back.at[w] if sending else back.at[here]
        return to_seq(src, dst, q1_s.at[j], q1_r.at[j], seq_uw(u, there))

    def q1_start(core):
        each(1, SIDE, lambda j: q1(j, True, core).start())

        def keep(i):
            back[w, i] = answer[w, i] if core == 0 else answer[i, w]

        each(0, SIDE, keep)

    by_core(q1_start)


    ring_step(3, 0)
    ring_step(3, 1)

    each(1, SIDE, lambda j: q1(j, False, 0).wait_recv())

    def q2(j, sending):
        there, here = rem(u + j, SIDE), rem(u + SIDE - j, SIDE)
        dst = final.at[u] if sending else final.at[here]
        return to_seq(back.at[:, there], dst, q2_s.at[j], q2_r.at[j], seq_uw(there, w))

    each(1, SIDE, lambda j: q2(j, True).start())

    def keep_final(i):
        final[u, i] = back[i, u]

    each(0, SIDE, keep_final)

    ring_step(4, 0)
    ring_step(4, 1)

    def project(e, zh):
        for part in range(2):
            first = (part * 16 + 4) * HD
            wide = jnp.concatenate([acts[2 * part], acts[2 * part + 1]], axis=1)
            at = pl.ds(first, 2 * LOCAL * HD)
            if part == 0:
                rows = wt[e, :, :, :, at]
            else:
                rows = wt[:, pl.ds(zh * 4, 4), :, :, at]
            share = dot(wide, rows.reshape(512, 2 * LOCAL * HD), NT)
            for n in range(2):
                piece = share[:, n * 256 : (n + 1) * 256]
                if part == 0:
                    summed[0, e, n] = piece
                else:
                    summed[1, n, zh] = piece

    each(1, SIDE, lambda j: q2(j, False).wait_recv())
    tokens = dot(place[...], final[...].reshape(1024, HD), TN).astype(BF)
    picked[0] = tokens[:TOK]
    picked[1] = tokens[TOK:]

    def xr(j, b, sending):
        there, here = rem(h + j, GROUPS), rem(h + GROUPS - j, GROUPS)
        own_side = c * (1 - b) + oc * b
        to = s * (1 - b) + sibling * b
        if sending:
            src, dst = picked.at[own_side], routed_acts.at[h, c]
        else:
            src, dst = picked.at[0], routed_acts.at[here, own_side]
        return to_any(src, dst, xr_s.at[j, b], xr_r.at[j, b], to, there if sending else here)

    for j in range(GROUPS):
        for b in range(2):
            if j or b:
                xr(j, b, True).start()
    routed_acts[h, c] = picked[c]

    for k in range(SIDE // 2):
        sib_wait(k)
    each(1, GROUPS, lambda j: xl(j, False).wait_recv())
    project(div(y, 4), div(z, 4))

    ring_step(5, 0)
    ring_step(5, 1)
    sib_wait(4)
    project(1 - div(y, 4), 1 - div(z, 4))
    for j in range(GROUPS):
        for b in range(2):
            if j or b:
                xr(j, b, False).wait_recv()
    wide = [
        jnp.concatenate([routed_acts[2 * part + g, n] for g in range(2) for n in range(2)], axis=1)
        for part in range(2)
    ]
    for e in range(2):
        for zh in range(2):
            total = summed[0, e, zh] + summed[1, e, zh]
            for part in range(2):
                first = part * 16 * HD
                rows = wt[e, 4 * zh : 4 * zh + 4, :, :, first : first + 4 * HD].reshape(256, 4 * HD)
                total = total + dot(wide[part], rows, NT)
            first = e * 512 + zh * 256
            out[:, first : first + 256] = total.astype(BF)

    for copy in a0(c):
        copy.wait_send()

    @pl.when(s < 2 * SIDE * SIDE - 1)
    def _():
        halo_copy.wait_send()

    for r in range(2):

        @pl.when(jnp.logical_not(target_is_me(r)))
        def _():
            for piece in range(2):
                w_send(r, piece).wait_send()

    def left(j):
        p1(j, True).wait_send()
        q2(j, True).wait_send()

    each(1, SIDE, left)

    def drain(core):
        def left(j):
            p2(j, True, core).wait_send()
            q1(j, True, core).wait_send()

        each(1, SIDE, left)

        each(1, SIDE, lambda j: w1(j, core, True).wait_send())

        for k in range(1, SIDE // 2 + 1):
            for part in range(2):
                for way in goes(k, part, core):
                    ring(k, way, part, core, True).wait_send()
        for k in range(SIDE // 2 + 1):
            for way in ways(k):
                sib(k, way, core).wait_send()

    by_core(drain)
    each(1, GROUPS, lambda j: xl(j, True).wait_send())
    for j in range(GROUPS):
        for b in range(2):
            if j or b:
                xr(j, b, True).wait_send()


def on_device(routed_qkv, local_qkv, cluster_ids, wo_routed, wo_local):
    sems = [
        (7,), (4,), (4,), (), (), (2, 2), (2, 2), (8,), (8,), (8,), (8,), (8,), (8,),
        (5, 2, 2), (5, 2, 2), (5, 2), (5, 2), (8,), (8,), (8,), (8,),
        (4,), (4,), (4, 2), (4, 2),
    ]
    scratch = [
        pltpu.VMEM((2, TOK, 4 * HD), BF),
        pltpu.VMEM((2, 1, TOK), I32),
        pltpu.VMEM((3, TOK, LOCAL * HD), BF),
        pltpu.VMEM((1024, 2 * TOK), BF),
        pltpu.VMEM((8, 8, 16, 3 * HD), BF),
        pltpu.VMEM((8, 8, 16, 3 * HD), BF),
        pltpu.VMEM((8, 8, 16, 3 * HD), BF),
        pltpu.VMEM((8, 8, 16, HD), BF),
        pltpu.VMEM((8, 8, 16, HD), BF),
        pltpu.VMEM((8, 8, 16, HD), BF),
        pltpu.VMEM((2, TOK, HD), BF),
        pltpu.VMEM((GROUPS, TOK, LOCAL * HD), BF),
        pltpu.VMEM((GROUPS, 2, TOK, HD), BF),
        pltpu.VMEM((2, TOK, LOCAL * HD), BF),
        pltpu.VMEM((2, 8, 4, 16, 32 * HD), BF),
        pltpu.VMEM((2, 2, 2, TOK, 256), F32),
    ]
    scratch += [pltpu.SemaphoreType.DMA(shape) if shape else pltpu.SemaphoreType.DMA for shape in sems]
    return pl.pallas_call(
        kernel,
        out_shape=jax.ShapeDtypeStruct((TOK, 1024), BF),
        in_specs=[pl.BlockSpec(memory_space=pltpu.HBM)] * 5,
        out_specs=pl.BlockSpec(memory_space=pltpu.VMEM),
        scratch_shapes=scratch,
        compiler_params=pltpu.CompilerParams(
            collective_id=0, has_side_effects=True, vmem_limit_bytes=60 * 2**20
        ),
        cost_estimate=pl.CostEstimate(flops=4 * 10**9, bytes_accessed=3 * 2**20, transcendentals=2 * 10**6),
    )(routed_qkv, local_qkv, cluster_ids.transpose(0, 2, 1), wo_routed.T, wo_local.T)


def solution(mesh):
    placed = (
        P(None, "seq", "head"),
        P(None, "seq", "head"),
        P("head", "seq", None),
        P("head", "seq"),
        P("head", "seq"),
    )
    return jax.shard_map(
        on_device, mesh=mesh, in_specs=placed, out_specs=P("seq", "head"), check_vma=False
    )
```

```python
import functools
import math

import jax
import jax.numpy as jnp
from jax import lax
from jax.experimental import pallas as pl
from jax.experimental.pallas import tpu as pltpu
from jax.sharding import PartitionSpec as P

HD = 128
TOK = 256
LOCAL = 6
SIDE = 8
GROUPS = 4
BOTH_WAYS = (4, 3, 5, 2, 6, 1, 7)
EMPTY = 128.0
NEVER = -1e30
SCALE = 1.0 / math.sqrt(HD)
BF = jnp.bfloat16
F32 = jnp.float32
I32 = jnp.int32
NT = (((1,), (1,)), ((), ()))
NN = (((1,), (0,)), ((), ()))
TN = (((0,), (0,)), ((), ()))


def dot(a, b, dims):
    return lax.dot_general(a, b, dims, preferred_element_type=F32)


def iota(shape, axis):
    return lax.broadcasted_iota(I32, shape, axis)


def each(low, high, body):
    for j in BOTH_WAYS if (low, high) == (1, SIDE) else range(low, high):
        body(j)


def div(a, b):
    if isinstance(a, int):
        return a // b
    return lax.div(a, jnp.int32(b))


def rem(a, b):
    if isinstance(a, int):
        return a % b
    return lax.rem(a, jnp.int32(b))


def kernel(
    routed, local_in, ids, wr, wl, out,
    own_x, own_ids, local, place, sent, via, got, answer, back, final, picked, acts, routed_acts, halo,
    wt, summed,
    in_s, a0_s, a0_r, halo_s, halo_r, wx_s, wx_r, p1_s, p1_r, p2_s, p2_r, w1_s, w1_r,
    ring_s, ring_r, sib_s, sib_r, q1_s, q1_r, q2_s, q2_r, xl_s, xl_r, xr_s, xr_r,
):
    h = lax.axis_index("head")
    s = lax.axis_index("seq")
    c = rem(s, 2)
    oc = 1 - c
    chip = div(s, 2)
    z = rem(chip, SIDE)
    y = div(chip, SIDE)
    u = z * oc + y * c
    w = y * oc + z * c
    sibling = s + 1 - 2 * c

    def seq_yz(yy, zz):
        return (yy * SIDE + zz) * 2 + c

    def seq_uw(uu, ww):
        return seq_yz(ww * oc + uu * c, uu * oc + ww * c)

    def to_seq(src, dst, ss, rs, seq):
        return pltpu.make_async_remote_copy(
            src_ref=src, dst_ref=dst, send_sem=ss, recv_sem=rs,
            device_id={"seq": seq}, device_id_type=pl.DeviceIdType.MESH,
        )

    def to_any(src, dst, ss, rs, seq, head):
        return pltpu.make_async_remote_copy(
            src_ref=src, dst_ref=dst, send_sem=ss, recv_sem=rs,
            device_id={"seq": seq, "head": head}, device_id_type=pl.DeviceIdType.MESH,
        )

    def hello(seq, head):
        pl.semaphore_signal(
            barrier, inc=1, device_id={"seq": seq, "head": head}, device_id_type=pl.DeviceIdType.MESH
        )

    def w_target(r):
        return div(y, 2), rem(y, 2) * 4 + c * 2 + r, div(h, 2)

    def w_source(i):
        return 2 * c + i, 2 * h + div(y, 4), div(rem(y, 4), 2)

    def target_is_me(r):
        head, row, core = w_target(r)
        return (head == h) & (row == y) & (core == c)

    def source_is_me(i):
        head, row, core = w_source(i)
        return (head == h) & (row == y) & (core == c)

    barrier = pltpu.get_barrier_semaphore()

    def greet(j):
        for target in (seq_uw(rem(u + j, SIDE), w), seq_uw(u, rem(w + j, SIDE))):
            pl.semaphore_signal(barrier, inc=1, device_id={"seq": target}, device_id_type=pl.DeviceIdType.MESH)

    each(1, SIDE, greet)
    pl.semaphore_signal(barrier, inc=1, device_id={"seq": sibling}, device_id_type=pl.DeviceIdType.MESH)
    for j in range(1, GROUPS):
        hello(s, rem(h + j, GROUPS))
        hello(sibling, rem(h + j, GROUPS))
    for i in range(2):
        head, row, core = w_source(i)

        @pl.when(jnp.logical_not(source_is_me(i)))
        def _():
            hello((row * SIDE + z) * 2 + core, head)

    @pl.when((c == 0) & (s > 0))
    def _():
        pl.semaphore_signal(barrier, inc=1, device_id={"seq": s - 1}, device_id_type=pl.DeviceIdType.MESH)

    selves = jnp.where(target_is_me(0) | target_is_me(1), 1, 0)
    expected = 2 * (SIDE - 1) + 1 + 2 * (GROUPS - 1) + 2
    pl.semaphore_wait(barrier, expected + c * (1 - div(s, 2 * SIDE * SIDE - 1)) - selves)

    def lanes(first, count):
        return pl.ds(pl.multiple_of(first, HD), count)

    halo_copy = to_seq(local_in.at[pl.ds(1, 2)], halo, halo_s, halo_r, s + 1)

    pieces = ((wr, 0, 2 * HD), (wl, 4 * HD, LOCAL * HD))

    def w_landing(row, head, piece):
        _, first, count = pieces[piece]
        at = lanes(div(head, 2) * 16 * HD + first + rem(head, 2) * count, count)
        return wt.at[div(row, 4), z, rem(row, 4), :, at]

    def w_send(r, piece):
        head, row, core = w_target(r)
        src = pieces[piece][0].at[pl.ds(r * 16, 16)]
        return to_any(
            src, w_landing(row, h, piece), wx_s.at[r, piece], wx_r.at[rem(h, 2), piece],
            (row * SIDE + z) * 2 + core, head,
        )

    def w_keep(r, piece):
        src = pieces[piece][0].at[pl.ds(r * 16, 16)]
        return pltpu.make_async_copy(src, w_landing(w_target(r)[1], h, piece), in_s.at[piece])

    def w_take(i, piece):
        head, row, core = w_source(i)
        src = pieces[piece][0].at[pl.ds(0, 16)]
        return to_any(
            src, w_landing(y, head, piece), wx_s.at[0, piece], wx_r.at[i, piece],
            (row * SIDE + z) * 2 + core, head,
        )

    for r in range(2):
        me = target_is_me(r)

        @pl.when(me)
        def _():
            for piece in range(2):
                w_keep(r, piece).start()

        @pl.when(jnp.logical_not(me))
        def _():
            for piece in range(2):
                w_send(r, piece).start()

    def head_rows(j, core):
        return routed.at[j, :, pl.ds(pl.multiple_of(core * HD, HD), HD)]

    def a0(core):
        copies = [
            to_seq(head_rows(j, oc), own_x.at[core, :, pl.ds(j * HD, HD)], a0_s.at[j], a0_r.at[j], sibling)
            for j in range(3)
        ]
        return copies + [to_seq(ids.at[oc], own_ids.at[core], a0_s.at[3], a0_r.at[3], sibling)]

    for copy in a0(c):
        copy.start()
    own = [
        pltpu.make_async_copy(head_rows(j, c), own_x.at[c, :, pl.ds(j * HD, HD)], in_s.at[2 + j])
        for j in range(3)
    ]
    own.append(pltpu.make_async_copy(ids.at[c], own_ids.at[c], in_s.at[5]))
    own.append(pltpu.make_async_copy(local_in, local, in_s.at[6]))
    for copy in own:
        copy.start()
    own_x[:, :, 3 * HD :] = jnp.ones((2, TOK, HD), BF)

    def block_of(core, yy, zz):
        return wt.at[div(yy, 4), zz, rem(yy, 4), :, pl.ds(core * 16 * HD, 16 * HD)]

    def w1(j, core, sending):
        if core == 0:
            target = seq_yz(y, rem(z + j, SIDE))
            here = rem(z + SIDE - j, SIDE)
            blk = block_of(core, y, z) if sending else block_of(core, y, here)
        else:
            target = seq_yz(rem(y + j, SIDE), z)
            here = rem(y + SIDE - j, SIDE)
            blk = block_of(core, y, z) if sending else block_of(core, here, z)
        return to_seq(blk, blk, w1_s.at[j], w1_r.at[j], target)

    def by_core(body):
        for core in range(2):
            pl.when(c == core)(functools.partial(body, core))

    for copy in own[:4]:
        copy.wait()
    for copy in a0(oc):
        copy.wait_recv()

    def rows_of(b):
        cluster = own_ids[b]
        name = cluster.astype(F32)
        first_row = jnp.where(iota((8, TOK), 0) == 0, jnp.broadcast_to(name, (8, TOK)), 0.0).astype(BF)
        down = dot(first_row, jnp.ones((8, TOK), BF), TN)
        earlier = (down == name) & (iota((TOK, TOK), 0) < iota((TOK, TOK), 1))
        rank = jnp.sum(jnp.where(earlier, 1.0, 0.0), axis=0, keepdims=True).astype(I32)
        owner = cluster >> 2
        turned = (owner & 7) * SIDE + (owner >> 3)
        goes = turned * oc + owner * c
        return goes * 16 + b * 8 + (cluster & 3) * 2 + rank

    slot = jnp.concatenate([rows_of(0), rows_of(1)], axis=1)
    both = own_x[...].reshape(2 * TOK, 4 * HD)

    def fill(i):
        hot = (iota((256, 2 * TOK), 0) + i * 256 == slot).astype(F32).astype(BF)
        place[pl.ds(i * 256, 256)] = hot
        rows = dot(hot, both, NN)
        lead = (1.0 - rows[:, 3 * HD :]) * EMPTY
        rows = jnp.concatenate([rows[:, :HD], rows[:, HD : 2 * HD] + lead, rows[:, 2 * HD : 3 * HD]], axis=1)
        sent[pl.ds(2 * i, 2)] = rows.astype(BF).reshape(2, SIDE, 16, 3 * HD)

    each(0, 4, fill)

    def p1(j, sending):
        there, here = rem(u + j, SIDE), rem(u + SIDE - j, SIDE)
        dst = via.at[u] if sending else via.at[here]
        return to_seq(sent.at[there], dst, p1_s.at[j], p1_r.at[j], seq_uw(there, w))

    each(1, SIDE, lambda j: p1(j, True).start())
    via[u] = sent[u]

    for i in range(2):
        me = source_is_me(i)
        for piece in range(2):

            @pl.when(me)
            def _():
                r = rem(y, 2)
                for value in range(2):

                    @pl.when(r == value)
                    def _():
                        w_keep(value, piece).wait()

            @pl.when(jnp.logical_not(me))
            def _():
                w_take(i, piece).wait_recv()

    def w1_start(core):
        each(1, SIDE, lambda j: w1(j, core, True).start())

    by_core(w1_start)

    @pl.when(s < 2 * SIDE * SIDE - 1)
    def _():
        halo_copy.start()


    def w1_take(core):
        each(1, SIDE, lambda j: w1(j, core, False).wait_recv())

    by_core(w1_take)

    def blocks(core, place_on, first=0, count=16 * HD):
        at = rem(place_on + SIDE, SIDE)
        part = pl.ds(core * 16 * HD + first, count)
        if core == 0:
            return wt.at[div(at, 4), :, rem(at, 4), :, part]
        return wt.at[:, at, :, :, part]

    def ring(k, way, part, core, sending):
        coord = y if core == 0 else z
        sign = 1 - 2 * way
        at = coord - sign * (k - 1) if sending else coord - sign * k
        blk = blocks(core, at, part * 8 * HD, 8 * HD)
        to = rem(coord + sign + SIDE, SIDE)
        target = seq_yz(to, z) if core == 0 else seq_yz(y, to)
        return to_seq(blk, blk, ring_s.at[k, way, part], ring_r.at[k, way, part], target)

    def goes(k, part, core):
        if k < SIDE // 2:
            return (0, 1)
        return (part,) if core == 0 else (1,)

    def sib(k, way, path):
        coord = y if path == 0 else z
        blk = blocks(path, coord - (1 - 2 * way) * k)
        return to_seq(blk, blk, sib_s.at[k, way], sib_r.at[k, way], sibling)

    def ways(k):
        return (0,) if k in (0, SIDE // 2) else (0, 1)

    def ring_step(k, part):
        def body(core):
            if k > 1:
                for way in goes(k - 1, part, core):
                    ring(k - 1, way, part, core, False).wait_recv()
            if k <= SIDE // 2:
                for way in goes(k, part, core):
                    ring(k, way, part, core, True).start()
            if part == 1:
                for way in ways(k - 1):
                    sib(k - 1, way, core).start()

        by_core(body)

    def sib_wait(k):
        def body(core):
            for way in ways(k):
                sib(k, way, 1 - core).wait_recv()

        by_core(body)

    ring_step(1, 0)
    ring_step(1, 1)

    each(1, SIDE, lambda j: p1(j, False).wait_recv())

    def p2(j, sending, core):
        there, here = rem(w + j, SIDE), rem(w + SIDE - j, SIDE)
        at = w if sending else here
        dst = got.at[at] if core == 0 else got.at[:, at]
        return to_seq(via.at[:, there], dst, p2_s.at[j], p2_r.at[j], seq_uw(u, there))

    def p2_start(core):
        each(1, SIDE, lambda j: p2(j, True, core).start())

        def keep(i):
            if core == 0:
                got[w, i] = via[i, w]
            else:
                got[i, w] = via[i, w]

        each(0, SIDE, keep)

    by_core(p2_start)
    ring_step(2, 0)
    ring_step(2, 1)

    own[4].wait()

    @pl.when(s > 0)
    def _():
        halo_copy.wait_recv()

    @pl.when(s == 0)
    def _():
        halo[...] = jnp.zeros_like(halo)

    own_side = iota((TOK, TOK), 1) <= iota((TOK, TOK), 0)
    shift = jnp.where(s > 0, jnp.float32(0.0), jnp.float32(NEVER))

    def window(n):
        cols = pl.ds(n * HD, HD)
        query = local[0, :, cols]
        here = dot(query, local[1, :, cols], NT) * SCALE
        before = dot(query, halo[0, :, cols], NT) * SCALE + shift
        scores = jnp.where(own_side, here, before)
        raised = jnp.exp(scores - jnp.max(scores, axis=1, keepdims=True))
        weights = raised * (1.0 / jnp.sum(raised, axis=1, keepdims=True))
        near = jnp.where(own_side, weights, 0.0).astype(BF)
        far = jnp.where(own_side, 0.0, weights).astype(BF)
        result = dot(near, local[2, :, cols], NN) + dot(far, halo[1, :, cols], NN)
        acts[h, :, pl.ds(n * HD, HD)] = result.astype(BF)

    each(0, LOCAL, window)

    def xl(j, sending):
        there, here = rem(h + j, GROUPS), rem(h + GROUPS - j, GROUPS)
        dst = acts.at[h] if sending else acts.at[here]
        return to_any(acts.at[h], dst, xl_s.at[j], xl_r.at[j], s, there)

    each(1, GROUPS, lambda j: xl(j, True).start())


    def p2_take(core):
        each(1, SIDE, lambda j: p2(j, False, core).wait_recv())

    by_core(p2_take)

    def code_of(r):
        return ((r >> 1) & 3) * 4096 + (r >> 4) * 4 + ((r >> 3) & 1) * 2 + (r & 1)

    keys = got[:, :, :, HD : 2 * HD].reshape(1024, HD)
    lane_zero = (iota((8, HD), 1) == 0).astype(F32).astype(BF)
    lead_key = dot(lane_zero, keys, NT)[0:1]
    key_code = jnp.where(lead_key < 0.75 * EMPTY, code_of(iota((8, 1024), 1))[0:1], 1 << 20)

    def cluster_rows(last, i):
        keys = got[: last // 128, :, :, HD : 2 * HD].reshape(last, HD)
        values = got[: last // 128, :, :, 2 * HD :].reshape(last, HD)
        query = got[pl.ds(2 * i, 2), :, :, 0:HD].reshape(256, HD)
        scores = dot(query, keys, NT) * SCALE
        ahead = code_of(iota((256, HD), 0) + i * 256)[:, 0:1] - key_code[:, :last]
        scores = jnp.where((ahead >= 0) & (ahead < 256), scores, NEVER)
        raised = jnp.exp(scores - jnp.max(scores, axis=1, keepdims=True))
        result = dot(raised.astype(BF), values, NN) * (1.0 / jnp.sum(raised, axis=1, keepdims=True))
        answer[pl.ds(2 * i, 2)] = result.astype(BF).reshape(2, SIDE, 16, HD)

    for i in range(4):
        cluster_rows((i + 1) * 256, i)

    def q1(j, sending, core):
        there, here = rem(w + j, SIDE), rem(w + SIDE - j, SIDE)
        src = answer.at[there] if core == 0 else answer.at[:, there]
        dst = back.at[w] if sending else back.at[here]
        return to_seq(src, dst, q1_s.at[j], q1_r.at[j], seq_uw(u, there))

    def q1_start(core):
        each(1, SIDE, lambda j: q1(j, True, core).start())

        def keep(i):
            back[w, i] = answer[w, i] if core == 0 else answer[i, w]

        each(0, SIDE, keep)

    by_core(q1_start)


    ring_step(3, 0)
    ring_step(3, 1)

    each(1, SIDE, lambda j: q1(j, False, 0).wait_recv())

    def q2(j, sending):
        there, here = rem(u + j, SIDE), rem(u + SIDE - j, SIDE)
        dst = final.at[u] if sending else final.at[here]
        return to_seq(back.at[:, there], dst, q2_s.at[j], q2_r.at[j], seq_uw(there, w))

    each(1, SIDE, lambda j: q2(j, True).start())

    def keep_final(i):
        final[u, i] = back[i, u]

    each(0, SIDE, keep_final)

    ring_step(4, 0)
    ring_step(4, 1)

    def project(e, zh):
        for part in range(2):
            first = (part * 16 + 4) * HD
            wide = jnp.concatenate([acts[2 * part], acts[2 * part + 1]], axis=1)
            at = pl.ds(first, 2 * LOCAL * HD)
            if part == 0:
                rows = wt[e, :, :, :, at]
            else:
                rows = wt[:, pl.ds(zh * 4, 4), :, :, at]
            share = dot(wide, rows.reshape(512, 2 * LOCAL * HD), NT)
            for n in range(2):
                piece = share[:, n * 256 : (n + 1) * 256]
                if part == 0:
                    summed[0, e, n] = piece
                else:
                    summed[1, n, zh] = piece

    each(1, SIDE, lambda j: q2(j, False).wait_recv())
    tokens = dot(place[...], final[...].reshape(1024, HD), TN).astype(BF)
    picked[0] = tokens[:TOK]
    picked[1] = tokens[TOK:]

    def xr(j, b, sending):
        there, here = rem(h + j, GROUPS), rem(h + GROUPS - j, GROUPS)
        own_side = c * (1 - b) + oc * b
        to = s * (1 - b) + sibling * b
        if sending:
            src, dst = picked.at[own_side], routed_acts.at[h, c]
        else:
            src, dst = picked.at[0], routed_acts.at[here, own_side]
        return to_any(src, dst, xr_s.at[j, b], xr_r.at[j, b], to, there if sending else here)

    for j in range(GROUPS):
        for b in range(2):
            if j or b:
                xr(j, b, True).start()
    routed_acts[h, c] = picked[c]

    for k in range(SIDE // 2):
        sib_wait(k)
    each(1, GROUPS, lambda j: xl(j, False).wait_recv())
    project(div(y, 4), div(z, 4))

    ring_step(5, 0)
    ring_step(5, 1)
    sib_wait(4)
    project(1 - div(y, 4), 1 - div(z, 4))
    for j in range(GROUPS):
        for b in range(2):
            if j or b:
                xr(j, b, False).wait_recv()
    wide = [
        jnp.concatenate([routed_acts[2 * part + g, n] for g in range(2) for n in range(2)], axis=1)
        for part in range(2)
    ]
    for e in range(2):
        for zh in range(2):
            total = summed[0, e, zh] + summed[1, e, zh]
            for part in range(2):
                first = part * 16 * HD
                rows = wt[e, 4 * zh : 4 * zh + 4, :, :, first : first + 4 * HD].reshape(256, 4 * HD)
                total = total + dot(wide[part], rows, NT)
            first = e * 512 + zh * 256
            out[:, first : first + 256] = total.astype(BF)

    for copy in a0(c):
        copy.wait_send()

    @pl.when(s < 2 * SIDE * SIDE - 1)
    def _():
        halo_copy.wait_send()

    for r in range(2):

        @pl.when(jnp.logical_not(target_is_me(r)))
        def _():
            for piece in range(2):
                w_send(r, piece).wait_send()

    def left(j):
        p1(j, True).wait_send()
        q2(j, True).wait_send()

    each(1, SIDE, left)

    def drain(core):
        def left(j):
            p2(j, True, core).wait_send()
            q1(j, True, core).wait_send()

        each(1, SIDE, left)

        each(1, SIDE, lambda j: w1(j, core, True).wait_send())

        for k in range(1, SIDE // 2 + 1):
            for part in range(2):
                for way in goes(k, part, core):
                    ring(k, way, part, core, True).wait_send()
        for k in range(SIDE // 2 + 1):
            for way in ways(k):
                sib(k, way, core).wait_send()

    by_core(drain)
    each(1, GROUPS, lambda j: xl(j, True).wait_send())
    for j in range(GROUPS):
        for b in range(2):
            if j or b:
                xr(j, b, True).wait_send()


def on_device(routed_qkv, local_qkv, cluster_ids, wo_routed, wo_local):
    sems = [
        (7,), (4,), (4,), (), (), (2, 2), (2, 2), (8,), (8,), (8,), (8,), (8,), (8,),
        (5, 2, 2), (5, 2, 2), (5, 2), (5, 2), (8,), (8,), (8,), (8,),
        (4,), (4,), (4, 2), (4, 2),
    ]
    scratch = [
        pltpu.VMEM((2, TOK, 4 * HD), BF),
        pltpu.VMEM((2, 1, TOK), I32),
        pltpu.VMEM((3, TOK, LOCAL * HD), BF),
        pltpu.VMEM((1024, 2 * TOK), BF),
        pltpu.VMEM((8, 8, 16, 3 * HD), BF),
        pltpu.VMEM((8, 8, 16, 3 * HD), BF),
        pltpu.VMEM((8, 8, 16, 3 * HD), BF),
        pltpu.VMEM((8, 8, 16, HD), BF),
        pltpu.VMEM((8, 8, 16, HD), BF),
        pltpu.VMEM((8, 8, 16, HD), BF),
        pltpu.VMEM((2, TOK, HD), BF),
        pltpu.VMEM((GROUPS, TOK, LOCAL * HD), BF),
        pltpu.VMEM((GROUPS, 2, TOK, HD), BF),
        pltpu.VMEM((2, TOK, LOCAL * HD), BF),
        pltpu.VMEM((2, 8, 4, 16, 32 * HD), BF),
        pltpu.VMEM((2, 2, 2, TOK, 256), F32),
    ]
    scratch += [pltpu.SemaphoreType.DMA(shape) if shape else pltpu.SemaphoreType.DMA for shape in sems]
    return pl.pallas_call(
        kernel,
        out_shape=jax.ShapeDtypeStruct((TOK, 1024), BF),
        in_specs=[pl.BlockSpec(memory_space=pltpu.HBM)] * 5,
        out_specs=pl.BlockSpec(memory_space=pltpu.VMEM),
        scratch_shapes=scratch,
        compiler_params=pltpu.CompilerParams(
            collective_id=0, has_side_effects=True, vmem_limit_bytes=60 * 2**20
        ),
        cost_estimate=pl.CostEstimate(flops=4 * 10**9, bytes_accessed=3 * 2**20, transcendentals=2 * 10**6),
    )(routed_qkv, local_qkv, cluster_ids.transpose(0, 2, 1), wo_routed.T, wo_local.T)


def solution(mesh):
    placed = (
        P(None, "seq", "head"),
        P(None, "seq", "head"),
        P("head", "seq", None),
        P("head", "seq"),
        P("head", "seq"),
    )
    return jax.shard_map(
        on_device, mesh=mesh, in_specs=placed, out_specs=P("seq", "head"), check_vma=False
    )
```
